32 devices in a mesh: groups: 2 (over x), fsdp: 16 (over z, y, core).
Axes of the slice: x: 2, y: 2, z: 4, core: 2. Of those that a mesh axis runs over, the one named last changes fastest.
Arguments:
- fields: bfloat16 [512, 32, 1536], P(('groups', 'fsdp')), parts along dimension 0, may hold values from -60 to 60
- shifts: int32 [2], replicated, may hold values from 1 to 7, as said below
- in_weight: bfloat16 [1536, 2304], P('fsdp'), may hold values from -0.15625 to 0.15625
- out_weight: bfloat16 [768, 1536], P('fsdp'), may hold values from -0.21875 to 0.21875
- bias_table: float32 [12, 225], replicated, may hold values from -4 to 324
- cotangent: bfloat16 [512, 32, 1536], P(('groups', 'fsdp')), parts along dimension 0, may hold values from -18 to 18
Outputs:
- attended: bfloat16 [512, 32, 1536], P(('groups', 'fsdp')), parts along dimension 0
- fields_gradient: bfloat16 [512, 32, 1536], P(('groups', 'fsdp')), parts along dimension 0
- out_grad: float32 [1536, 1536], P(('groups', 'fsdp')), parts along dimension 0
- table_grad: float32 [24, 225], P('groups'), parts along dimension 0
The draws below stay inside these ranges and needn't reach their ends.
There are 2 independent parts, one for each index of `groups`. The reference program is written for one: setup_inputs(seed, part) draws one part's arguments, and reference() takes and returns one part's arrays. A program takes and returns all parts, laid end to end along the dimension named above; an argument that names none is the same for every part. Nothing has to cross between parts.
Inputs may be any that keep to these rules, and one draw needn't show every extreme that they name: The two shifts differ, and one of them is 7.
All inputs are finite; a program needn't handle non-finite values.
Results may differ from the reference program's by a relative error of at most 0.0095.
Values may be sent and summed in bfloat16 or wider, within the bound.
A program may use at most 128 MiB of HBM per device.

```python
import math
import jax
import jax.numpy as jnp
from jax import lax

D = 1536
HEADS = 12
HD = 64
WIN = 8
SIDE = 32
COLS = 32
SLICES = 8
ROWS = 256
HH = 768
REL = 225


def draw_fields(key, part):
    first, second, third = jax.random.split(jax.random.fold_in(key, 11), 3)
    base = jnp.clip(jax.random.normal(first, (ROWS, COLS, D), jnp.float32), -6.0, 6.0)
    row_scale = jnp.exp(jax.random.uniform(second, (ROWS, COLS, 1), jnp.float32, 0.0, math.log(10.0)))
    col_scale = jnp.exp(jax.random.uniform(third, (1, 1, D), jnp.float32, 0.0, math.log(10.0)))
    return (0.1 * base * row_scale * col_scale).astype(jnp.bfloat16)


def draw_shifts(key, part):
    first, second = jax.random.split(jax.random.fold_in(key, 41), 2)
    which = jax.random.randint(first, (), 0, 2, dtype=jnp.int32)
    other = jax.random.randint(second, (), 1, WIN - 1, dtype=jnp.int32)
    top = jnp.int32(WIN - 1)
    row_shift = jnp.where(which == 0, top, other)
    col_shift = jnp.where(which == 0, other, top)
    return jnp.stack([row_shift, col_shift]).astype(jnp.int32)


def draw_cotangent(key, part):
    first = jax.random.fold_in(key, 23)
    ramp = jnp.arange(ROWS, dtype=jnp.float32) / (ROWS - 1)
    base = jnp.clip(jax.random.normal(first, (ROWS, COLS, D), jnp.float32), -6.0, 6.0)
    rise = 1.0 + 2.0 * ramp
    return (base * rise[:, None, None]).astype(jnp.bfloat16)


def draw_bias_table(key, part):
    first = jax.random.fold_in(jax.random.fold_in(key, 37), 0)
    base = jnp.clip(jax.random.normal(first, (HEADS, REL), jnp.float32), -4.0, 4.0)
    return base


def level_of(own_key, shape, shards, low, largest):
    level, own = 1.0, jax.random.fold_in(own_key, 6)
    for dim, parts in shards:
        steps = jnp.exp(jax.random.uniform(jax.random.fold_in(own, dim), (parts,), jnp.float32, low / len(shards), largest / len(shards)))
        level = level * jnp.repeat(steps, shape[dim] // parts).reshape([-1 if axis == dim else 1 for axis in range(len(shape))])
    return level


def bell_draw(rng, shape, spread, bound, cuts=(), kind=jnp.bfloat16):
    array = jax.random.normal(rng, shape, jnp.float32) * spread
    if len(cuts) > 0:
        array = level_of(rng, shape, cuts, -0.22, 0.18) * array
    return jnp.clip(array, min=-bound, max=bound).astype(kind)


def setup_inputs(seed: int = 0, part: int = 0) -> dict:
    splits = jax.random.split(jax.random.key(seed), 7)
    part_splits = jax.random.split(jax.random.fold_in(splits[6], part), 7)
    fields = draw_fields(jax.random.fold_in(jax.random.fold_in(splits[6], part), 71), part)
    shifts = draw_shifts(jax.random.fold_in(splits[6], 71), part)
    in_weight = bell_draw(splits[2], (D, 3 * HH), D ** -0.5, 0.15625, ((0, 16),))
    out_weight = bell_draw(splits[3], (HH, D), HH ** -0.5, 0.21875, ((0, 16),))
    bias_table = draw_bias_table(jax.random.fold_in(splits[6], 71), part)
    cotangent = draw_cotangent(jax.random.fold_in(jax.random.fold_in(splits[6], part), 71), part)
    return {"fields": fields, "shifts": shifts, "in_weight": in_weight, "out_weight": out_weight, "bias_table": bias_table, "cotangent": cotangent}


def rounded(tensor):
    return lax.optimization_barrier(tensor.astype(jnp.bfloat16))

def layer_norm_statistics(fields):
    values = fields.astype(jnp.float32)
    centered = values - lax.optimization_barrier(jnp.mean(values, axis=-1, keepdims=True))
    inverse_scale = lax.rsqrt(lax.optimization_barrier(jnp.mean(centered * centered, axis=-1, keepdims=True)) + 1e-05)
    return (centered * inverse_scale, inverse_scale)

def region_labels(index, total, window, offset):
    return (index >= total - window).astype(jnp.int32) + (index >= total - offset).astype(jnp.int32)

def window_split(tensor, window):
    row_count = tensor.shape[0]
    col_count = tensor.shape[1]
    channels = tensor.shape[2]
    row_blocks = row_count // window
    col_blocks = col_count // window
    moved = tensor.reshape(row_blocks, window, col_blocks, window, channels).transpose(0, 2, 1, 3, 4)
    return moved.reshape(row_blocks * col_blocks, window * window, channels)

def window_join(tensor, window, row_count, col_count):
    channels = tensor.shape[2]
    row_blocks = row_count // window
    col_blocks = col_count // window
    moved = tensor.reshape(row_blocks, col_blocks, window, window, channels).transpose(0, 2, 1, 3, 4)
    return moved.reshape(row_count, col_count, channels)

def attend_block(shifted, cot_shifted, row_start, total_rows, in_weight, out_weight, bias_full, shift_h, shift_w):
    window = WIN
    col_count = shifted.shape[1]
    windows = col_count // window
    area = window * window
    inner = HEADS * HD
    score_scale = HD ** (-0.5)
    shifted_tok = shifted.reshape(window * col_count, D)
    packed = rounded(jnp.dot(shifted_tok, in_weight, preferred_element_type=jnp.float32))
    split_win = window_split(packed.reshape(window, col_count, 3 * inner), window)
    split_win = split_win.reshape(windows, area, 3, HEADS, HD).astype(jnp.float32)
    queries = split_win[:, :, 0]
    keyed = split_win[:, :, 1]
    valued = split_win[:, :, 2]
    scores = jnp.einsum('nqhd,nkhd->nhqk', queries, keyed) * score_scale + bias_full[None]
    row_label = region_labels(row_start + jnp.arange(window, dtype=jnp.int32), total_rows, window, shift_h)
    col_label = region_labels(jnp.arange(col_count, dtype=jnp.int32), col_count, window, shift_w)
    region = window_split((3 * row_label[:, None] + col_label[None, :])[:, :, None], window).reshape(windows, area)
    allowed = region[:, :, None] == region[:, None, :]
    scores = jnp.where(allowed[:, None], scores, -1000000000.0)
    top_score = lax.optimization_barrier(jnp.max(scores, axis=-1, keepdims=True))
    exp_scores = jnp.exp(scores - top_score)
    probability = exp_scores / lax.optimization_barrier(jnp.sum(exp_scores, axis=-1, keepdims=True))
    prob_low = rounded(probability).astype(jnp.float32)
    context = rounded(jnp.einsum('nhqk,nkhd->nqhd', prob_low, valued))
    context_tok = window_join(context.reshape(windows, area, inner), window, window, col_count).reshape(window * col_count, inner)
    projected = jnp.dot(context_tok, out_weight, preferred_element_type=jnp.float32).astype(jnp.bfloat16)
    projected = projected.reshape(window, col_count, D)
    cot_tok = cot_shifted.reshape(window * col_count, D)
    dcontext = rounded(lax.dot_general(cot_tok, out_weight, (((1,), (1,)), ((), ())), preferred_element_type=jnp.float32))
    dcontext_win = window_split(dcontext.reshape(window, col_count, inner), window)
    dcontext_win = dcontext_win.reshape(windows, area, HEADS, HD).astype(jnp.float32)
    dprob = jnp.einsum('nqhd,nkhd->nhqk', dcontext_win, valued)
    dvalued = jnp.einsum('nhqk,nqhd->nkhd', prob_low, dcontext_win)
    dscore = probability * (dprob - lax.optimization_barrier(jnp.sum(probability * dprob, axis=-1, keepdims=True)))
    dscore_low = rounded(dscore).astype(jnp.float32)
    dquery = jnp.einsum('nhqk,nkhd->nqhd', dscore_low, keyed) * score_scale
    dkeyed = jnp.einsum('nhqk,nqhd->nkhd', dscore_low, queries) * score_scale
    dpacked = rounded(jnp.stack([dquery, dkeyed, dvalued], axis=2))
    dpacked_tok = window_join(dpacked.reshape(windows, area, 3 * inner), window, window, col_count).reshape(window * col_count, 3 * inner)
    dshifted = lax.dot_general(dpacked_tok, in_weight, (((1,), (1,)), ((), ())), preferred_element_type=jnp.float32)
    dshifted = dshifted.astype(jnp.bfloat16).reshape(window, col_count, D)
    return (projected, dshifted, context_tok, lax.optimization_barrier(jnp.sum(dscore, axis=0)))

def slice_roll(tensor, shift_h, shift_w):
    sliced = tensor.reshape(SLICES, SIDE, COLS, D)
    return jnp.roll(sliced, (shift_h, shift_w), axis=(1, 2)).reshape(ROWS, COLS, D)

def reference(fields, shifts, in_weight, out_weight, bias_table, cotangent):
    window = WIN
    span = 2 * window - 1
    area = window * window
    standardized_input, inverse_scale = layer_norm_statistics(fields)
    normalized_input = standardized_input.astype(jnp.bfloat16)
    shift_h = shifts[0]
    shift_w = shifts[1]
    shifted = slice_roll(normalized_input, -shift_h, -shift_w)
    cot_shifted = slice_roll(cotangent, -shift_h, -shift_w)
    position = jnp.arange(area, dtype=jnp.int32)
    pos_row = position // window
    pos_col = position % window
    relative = (pos_row[:, None] - pos_row[None, :] + window - 1) * span + (pos_col[:, None] - pos_col[None, :] + window - 1)
    bias_full = bias_table[:, relative]
    blocks = ROWS // window
    shifted_blocks = shifted.reshape(blocks, window, COLS, D)
    cot_blocks = cot_shifted.reshape(blocks, window, COLS, D)

    def visit(carry, inputs):
        out_total, score_total = carry
        block_index, shifted_block, cot_block = inputs
        row_start = block_index * window % SIDE
        projected, dshifted, context_tok, dscore_sum = attend_block(shifted_block, cot_block, row_start, SIDE, in_weight, out_weight, bias_full, shift_h, shift_w)
        cot_tok = cot_block.reshape(window * COLS, D)
        out_total = out_total + lax.dot_general(context_tok, cot_tok, (((0,), (0,)), ((), ())), preferred_element_type=jnp.float32)
        return ((out_total, score_total + dscore_sum), (projected, dshifted))
    start = (jnp.zeros((HEADS * HD, D), jnp.float32), jnp.zeros((HEADS, area, area), jnp.float32))
    (out_grad, score_total), (projected, dshifted) = lax.scan(visit, start, (jnp.arange(blocks, dtype=jnp.int32), shifted_blocks, cot_blocks))
    attended = slice_roll(projected.reshape(ROWS, COLS, D), shift_h, shift_w)
    dnormed = slice_roll(dshifted.reshape(ROWS, COLS, D), shift_h, shift_w)
    value_gradient_rows = dnormed.astype(jnp.float32)
    average_gradient = lax.optimization_barrier(jnp.mean(value_gradient_rows, axis=-1, keepdims=True))
    average_cross_product = lax.optimization_barrier(jnp.mean(value_gradient_rows * standardized_input, axis=-1, keepdims=True))
    fields_gradient = (inverse_scale * (value_gradient_rows - average_gradient - standardized_input * average_cross_product)).astype(jnp.bfloat16)
    table_grad = jnp.zeros((HEADS, REL), jnp.float32).at[:, relative.reshape(-1)].add(score_total.reshape(HEADS, area * area))
    return (attended, fields_gradient, out_grad, table_grad)
```

```python
import functools

import jax
import jax.numpy as jnp
from jax import lax
from jax.experimental import pallas as pl
from jax.experimental.pallas import tpu as pltpu
from jax.sharding import PartitionSpec as P

HEADS = 12
HD = 64
WIN = 8
SIDE = 32
MINE = HEADS // 2
HALF = MINE * HD
BAND = WIN * SIDE
PAIR = 2 * WIN * WIN
BANDS = SIDE // WIN
VMEM_LIMIT = 60 * 1024 * 1024
F32 = jnp.float32
BF16 = jnp.bfloat16


def dot(a, b, dims=((1,), (0,))):
    return lax.dot_general(a, b, (dims, ((), ())), preferred_element_type=F32)


def partner(block):
    count = lax.axis_size("fsdp")
    return lax.ppermute(block, "fsdp", [(d, d ^ 1) for d in range(count)])


def same_core_groups():
    count = lax.axis_size("fsdp")
    return [list(range(0, count, 2)), list(range(1, count, 2))]


def band_permutation(shift_w):
    t = lax.broadcasted_iota(jnp.int32, (BAND, BAND), 0)
    s = lax.broadcasted_iota(jnp.int32, (BAND, BAND), 1)
    row = (t >> 3) & 7
    col = ((t >> 6) * WIN + (t & 7) + shift_w) & (SIDE - 1)
    return (row * SIDE + col == s).astype(F32).astype(BF16)


def pair_labels(band, pair, shift_h, shift_w, axis):
    shape = (PAIR, 1) if axis == 0 else (1, PAIR)
    t = lax.broadcasted_iota(jnp.int32, shape, axis)
    which = t >> 6
    row = band * WIN + ((t >> 3) & 7)
    col = pair * 2 * WIN + which * WIN + (t & 7)

    def label(index, shift):
        return jnp.where(index >= SIDE - WIN, 1, 0) + jnp.where(index >= SIDE - shift, 1, 0)

    return which * 16 + 3 * label(row, shift_h) + label(col, shift_w)


def read_band(ref, band, shift_h):
    rows = [ref[(band * WIN + i + shift_h) & (SIDE - 1)] for i in range(WIN)]
    return jnp.concatenate(rows, axis=0)


def write_band(ref, value, band, shift_h):
    for i in range(WIN):
        ref[(band * WIN + i + shift_h) & (SIDE - 1)] = value[i * SIDE : (i + 1) * SIDE]


def forward_kernel(
    shifts, x_ref, cot_ref, w_ref, ow_ref, bias_ref, packed_ref, prob_ref, dctx_ref, proj_ref, og_ref
):
    shift_h = shifts[0]
    shift_w = shifts[1]
    perm = band_permutation(shift_w)

    def body(band, _):
        tokens = pl.ds(pl.multiple_of(band * BAND, BAND), BAND)
        xs = dot(perm, read_band(x_ref, band, shift_h)).astype(BF16)
        packed = dot(xs, w_ref[...]).astype(BF16)
        packed_ref[tokens, :] = packed
        cot = dot(perm, read_band(cot_ref, band, shift_h)).astype(BF16)
        dctx_ref[tokens, :] = dot(cot, ow_ref[...], ((1,), (1,))).astype(BF16)
        pairs = []
        for pair in range(2):
            rows = slice(pair * PAIR, (pair + 1) * PAIR)
            allowed = pair_labels(band, pair, shift_h, shift_w, 0) == pair_labels(
                band, pair, shift_h, shift_w, 1
            )
            heads = []
            for h in range(MINE):
                q = packed[rows, h * HD : (h + 1) * HD]
                k = packed[rows, HALF + h * HD : HALF + (h + 1) * HD]
                v = packed[rows, 2 * HALF + h * HD : 2 * HALF + (h + 1) * HD]
                s = dot(q, k, ((1,), (1,))) * (HD**-0.5) + bias_ref[h]
                s = jnp.where(allowed, s, -1e9)
                e = jnp.exp(s - jnp.max(s, axis=-1, keepdims=True))
                p = e / jnp.sum(e, axis=-1, keepdims=True)
                prob_ref[(band * 2 + pair) * MINE + h] = p
                heads.append(dot(p.astype(BF16), v).astype(BF16))
            pairs.append(jnp.concatenate(heads, axis=1))
        ctx = jnp.concatenate(pairs, axis=0)
        grad = dot(ctx, cot, ((0,), (0,)))

        @pl.when(band == 0)
        def _():
            og_ref[...] = grad

        @pl.when(band > 0)
        def _():
            og_ref[...] += grad

        proj = dot(ctx, ow_ref[...]).astype(BF16)
        back = dot(perm, proj, ((0,), (0,))).astype(BF16)
        write_band(proj_ref, back, band, shift_h)
        return 0

    lax.fori_loop(0, BANDS, body, 0)


def backward_kernel(shifts, packed_ref, prob_ref, dctx_ref, w_ref, dn_ref, table_ref, dpk):
    shift_h = shifts[0]
    shift_w = shifts[1]
    perm = band_permutation(shift_w)
    scale = HD**-0.5
    table_ref[...] = jnp.zeros_like(table_ref)

    def body(band, _):
        for pair in range(2):
            rows = pl.ds(pl.multiple_of(band * BAND + pair * PAIR, PAIR), PAIR)
            packed = packed_ref[rows, :]
            dctx = dctx_ref[rows, :]
            dqs, dks, dvs = [], [], []
            for h in range(MINE):
                q = packed[:, h * HD : (h + 1) * HD]
                k = packed[:, HALF + h * HD : HALF + (h + 1) * HD]
                v = packed[:, 2 * HALF + h * HD : 2 * HALF + (h + 1) * HD]
                d = dctx[:, h * HD : (h + 1) * HD]
                p = prob_ref[(band * 2 + pair) * MINE + h]
                dp = dot(d, v, ((1,), (1,)))
                dvs.append(dot(p.astype(BF16), d, ((0,), (0,))).astype(BF16))
                ds = p * (dp - jnp.sum(p * dp, axis=-1, keepdims=True))
                table_ref[h] += ds
                low = ds.astype(BF16)
                dqs.append((dot(low, k) * scale).astype(BF16))
                dks.append((dot(low, q, ((0,), (0,))) * scale).astype(BF16))
            dpk[pair * PAIR : (pair + 1) * PAIR, :] = jnp.concatenate(dqs + dks + dvs, axis=1)
        dsh = dot(dpk[...], w_ref[...], ((1,), (1,))).astype(BF16)
        back = dot(perm, dsh, ((0,), (0,))).astype(BF16)
        write_band(dn_ref, back, band, shift_h)
        return 0

    lax.fori_loop(0, BANDS, body, 0)


def norm_kernel(x_ref, o_ref):
    values = x_ref[...].astype(F32)
    centered = values - jnp.mean(values, axis=-1, keepdims=True)
    scale = lax.rsqrt(jnp.mean(centered * centered, axis=-1, keepdims=True) + 1e-05)
    o_ref[...] = (centered * scale).astype(BF16)


def norm_back_kernel(x_ref, a_ref, b_ref, o_ref):
    values = x_ref[...].astype(F32)
    centered = values - jnp.mean(values, axis=-1, keepdims=True)
    scale = lax.rsqrt(jnp.mean(centered * centered, axis=-1, keepdims=True) + 1e-05)
    xhat = centered * scale
    grad = a_ref[...].astype(F32) + b_ref[...].astype(F32)
    grad = grad.astype(BF16).astype(F32)
    mean_grad = jnp.mean(grad, axis=-1, keepdims=True)
    mean_cross = jnp.mean(grad * xhat, axis=-1, keepdims=True)
    o_ref[...] = (scale * (grad - mean_grad - xhat * mean_cross)).astype(BF16)


def rowwise(kernel, *arrays):
    rows, cols, width = arrays[0].shape
    step = 4
    spec = pl.BlockSpec((step, cols, width), lambda i: (i, 0, 0))
    return pl.pallas_call(
        kernel,
        out_shape=jax.ShapeDtypeStruct(arrays[0].shape, BF16),
        grid=(rows // step,),
        in_specs=[spec] * len(arrays),
        out_specs=spec,
        cost_estimate=pl.CostEstimate(
            flops=20 * rows * cols * width, bytes_accessed=2 * rows * cols * width * 3, transcendentals=0
        ),
    )(*arrays)


def whole(count):
    return [pl.BlockSpec(memory_space=pltpu.VMEM)] * count


def shape(dims, kind):
    return jax.ShapeDtypeStruct(dims, kind)


def offset_table(window):
    span = 2 * window - 1
    position = jnp.arange(window, dtype=jnp.int32)
    offset = position[:, None] - position[None, :] + window - 1
    return (offset[:, :, None] == jnp.arange(span, dtype=jnp.int32)[None, None, :]).astype(F32)


def both_halves(own, other, core):
    return jnp.where(
        core == 0, jnp.concatenate([own, other], axis=0), jnp.concatenate([other, own], axis=0)
    )


def shards(fields, shifts, in_weight, out_weight, bias_table, cotangent):
    row_count, col_count, width = fields.shape
    core = lax.axis_index("fsdp") % 2
    chips = lax.axis_size("fsdp") // 2
    groups = same_core_groups()
    span = 2 * WIN - 1
    area = WIN * WIN

    split = in_weight.reshape(in_weight.shape[0], 3, 2, HALF)
    keep = lax.dynamic_index_in_dim(split, core, 2, False).reshape(-1, 3 * HALF)
    give = lax.dynamic_index_in_dim(split, 1 - core, 2, False).reshape(-1, 3 * HALF)
    w_chip = both_halves(keep, partner(give), core)
    w_full = lax.all_gather(w_chip, "fsdp", axis=0, tiled=True, axis_index_groups=groups)

    mine = lax.all_gather(out_weight, "fsdp", axis=0, tiled=False, axis_index_groups=groups)
    ow_keep = lax.dynamic_slice_in_dim(mine, core * (chips // 2), chips // 2, 0)
    ow_give = lax.dynamic_slice_in_dim(mine, (1 - core) * (chips // 2), chips // 2, 0)
    ow_got = partner(ow_give)
    ow_even = jnp.where(core == 0, ow_keep, ow_got)
    ow_odd = jnp.where(core == 0, ow_got, ow_keep)
    ow_full = jnp.stack([ow_even, ow_odd], axis=1).reshape(HALF, width)

    normed = rowwise(norm_kernel, fields)
    x_all = both_halves(normed, partner(normed), core)
    cot_all = both_halves(cotangent, partner(cotangent), core)

    table = offset_table(WIN)
    own_table = lax.dynamic_slice_in_dim(bias_table, core * MINE, MINE, 0)
    bias = jnp.einsum(
        "huv,pqu,rsv->hprqs",
        own_table.reshape(MINE, span, span),
        table,
        table,
        precision=lax.Precision.HIGHEST,
    ).reshape(MINE, area, area)
    bias = jnp.tile(bias, (1, 2, 2))

    tokens = SIDE * SIDE
    blocks = BANDS * 2 * MINE
    params = pltpu.CompilerParams(vmem_limit_bytes=VMEM_LIMIT)
    smem = pl.BlockSpec(memory_space=pltpu.SMEM)
    packed, prob, dctx, proj, og = pl.pallas_call(
        forward_kernel,
        out_shape=(
            shape((tokens, 3 * HALF), BF16),
            shape((blocks, PAIR, PAIR), F32),
            shape((tokens, HALF), BF16),
            shape((SIDE, SIDE, width), BF16),
            shape((HALF, width), F32),
        ),
        in_specs=[smem] + whole(5),
        out_specs=tuple(whole(5)),
        compiler_params=params,
        cost_estimate=pl.CostEstimate(flops=10**10, bytes_accessed=2 * 10**7, transcendentals=10**6),
    )(shifts, x_all, cot_all, w_full, ow_full, bias)

    rows = og.shape[0] // chips
    parts = og.reshape(chips // 2, 2, rows, width)
    og_keep = lax.dynamic_index_in_dim(parts, core, 1, False)
    og_got = partner(lax.dynamic_index_in_dim(parts, 1 - core, 1, False))
    og_all = both_halves(og_keep, og_got, core).reshape(chips * rows, width)
    out_grad = lax.psum_scatter(
        og_all, "fsdp", scatter_dimension=0, tiled=True, axis_index_groups=groups
    )

    dn, score = pl.pallas_call(
        backward_kernel,
        out_shape=(shape((SIDE, SIDE, width), BF16), shape((MINE, PAIR, PAIR), F32)),
        in_specs=[smem] + whole(4),
        out_specs=tuple(whole(2)),
        scratch_shapes=[pltpu.VMEM((BAND, 3 * HALF), BF16)],
        compiler_params=params,
        cost_estimate=pl.CostEstimate(flops=10**10, bytes_accessed=2 * 10**7, transcendentals=10**6),
    )(shifts, packed, prob, dctx, w_full)

    def swap_rows(full):
        own = lax.dynamic_slice_in_dim(full, core * row_count, row_count, 0)
        return own, partner(lax.dynamic_slice_in_dim(full, (1 - core) * row_count, row_count, 0))

    a_own, a_got = swap_rows(proj)
    attended = (a_own.astype(F32) + a_got.astype(F32)).astype(BF16)
    d_own, d_got = swap_rows(dn)
    fields_gradient = rowwise(norm_back_kernel, fields, d_own, d_got)

    local = (score[:, :area, :area] + score[:, area:, area:]).reshape(MINE, WIN, WIN, WIN, WIN)
    own_grad = jnp.einsum(
        "hprqs,pqu,rsv->huv", local, table, table, precision=lax.Precision.HIGHEST
    ).reshape(MINE, span * span)
    padded = lax.dynamic_update_slice_in_dim(
        jnp.zeros((HEADS, span * span), F32), own_grad, core * MINE, 0
    )
    table_grad = lax.psum(padded, "fsdp")
    return (attended, fields_gradient, out_grad, table_grad)


def solution(mesh):
    in_specs = (
        P(("groups", "fsdp"), None, None),
        P(),
        P("fsdp", None),
        P("fsdp", None),
        P(),
        P(("groups", "fsdp"), None, None),
    )
    out_specs = (
        P(("groups", "fsdp"), None, None),
        P(("groups", "fsdp"), None, None),
        P(("groups", "fsdp"), None),
        P("groups", None),
    )
    return jax.shard_map(shards, mesh=mesh, in_specs=in_specs, out_specs=out_specs, check_vma=False)
```

```python
import functools

import jax
import jax.numpy as jnp
from jax import lax
from jax.experimental import pallas as pl
from jax.experimental.pallas import tpu as pltpu
from jax.sharding import PartitionSpec as P

HEADS = 12
HD = 64
WIN = 8
SIDE = 32
MINE = HEADS // 2
HALF = MINE * HD
BAND = WIN * SIDE
PAIR = 2 * WIN * WIN
BANDS = SIDE // WIN
VMEM_LIMIT = 60 * 1024 * 1024
F32 = jnp.float32
BF16 = jnp.bfloat16


def dot(a, b, dims=((1,), (0,))):
    return lax.dot_general(a, b, (dims, ((), ())), preferred_element_type=F32)


def partner(block):
    count = lax.axis_size("fsdp")
    return lax.ppermute(block, "fsdp", [(d, d ^ 1) for d in range(count)])


def same_core_groups():
    count = lax.axis_size("fsdp")
    return [list(range(0, count, 2)), list(range(1, count, 2))]


def band_permutation(shift_w):
    t = lax.broadcasted_iota(jnp.int32, (BAND, BAND), 0)
    s = lax.broadcasted_iota(jnp.int32, (BAND, BAND), 1)
    row = (t >> 3) & 7
    col = ((t >> 6) * WIN + (t & 7) + shift_w) & (SIDE - 1)
    return (row * SIDE + col == s).astype(F32).astype(BF16)


def pair_labels(band, pair, shift_h, shift_w, axis):
    shape = (PAIR, 1) if axis == 0 else (1, PAIR)
    t = lax.broadcasted_iota(jnp.int32, shape, axis)
    which = t >> 6
    row = band * WIN + ((t >> 3) & 7)
    col = pair * 2 * WIN + which * WIN + (t & 7)

    def label(index, shift):
        return jnp.where(index >= SIDE - WIN, 1, 0) + jnp.where(index >= SIDE - shift, 1, 0)

    return which * 16 + 3 * label(row, shift_h) + label(col, shift_w)


def read_band(ref, band, shift_h):
    rows = [ref[(band * WIN + i + shift_h) & (SIDE - 1)] for i in range(WIN)]
    return jnp.concatenate(rows, axis=0)


def write_band(own_ref, give_ref, value, band, shift_h, core):
    half = SIDE // 2
    for i in range(WIN):
        row = (band * WIN + i + shift_h) & (SIDE - 1)
        inside = row & (half - 1)
        mine = row // half == core

        @pl.when(mine)
        def _():
            own_ref[inside] = value[i * SIDE : (i + 1) * SIDE]

        @pl.when(jnp.logical_not(mine))
        def _():
            give_ref[inside] = value[i * SIDE : (i + 1) * SIDE]


def forward_kernel(
    shifts, x_ref, cot_ref, w_ref, ow_ref, bias_ref, packed_ref, prob_ref, dctx_ref, own_ref, give_ref, og_out, og_ref
):
    shift_h = shifts[0]
    shift_w = shifts[1]
    core = shifts[2]
    perm = band_permutation(shift_w)
    ow = ow_ref.at[pl.ds(pl.multiple_of(core * HALF, HALF), HALF), :]

    def body(band, _):
        tokens = pl.ds(pl.multiple_of(band * BAND, BAND), BAND)
        xs = dot(perm, read_band(x_ref, band, shift_h)).astype(BF16)
        packed = dot(xs, w_ref[...]).astype(BF16)
        packed_ref[tokens, :] = packed
        cot = dot(perm, read_band(cot_ref, band, shift_h)).astype(BF16)
        dctx_ref[tokens, :] = dot(cot, ow[...], ((1,), (1,))).astype(BF16)
        pairs = []
        for pair in range(2):
            rows = slice(pair * PAIR, (pair + 1) * PAIR)
            allowed = pair_labels(band, pair, shift_h, shift_w, 0) == pair_labels(
                band, pair, shift_h, shift_w, 1
            )
            heads = []
            for h in range(MINE):
                q = packed[rows, h * HD : (h + 1) * HD]
                k = packed[rows, HALF + h * HD : HALF + (h + 1) * HD]
                v = packed[rows, 2 * HALF + h * HD : 2 * HALF + (h + 1) * HD]
                s = dot(q, k, ((1,), (1,))) * (HD**-0.5) + bias_ref[h]
                s = jnp.where(allowed, s, -1e9)
                e = jnp.exp(s - jnp.max(s, axis=-1, keepdims=True))
                p = e / jnp.sum(e, axis=-1, keepdims=True)
                prob_ref[(band * 2 + pair) * MINE + h] = p
                heads.append(dot(p.astype(BF16), v).astype(BF16))
            pairs.append(jnp.concatenate(heads, axis=1))
        ctx = jnp.concatenate(pairs, axis=0)
        grad = dot(ctx, cot, ((0,), (0,)))

        @pl.when(band == 0)
        def _():
            og_ref[...] = grad.reshape(og_ref.shape)

        @pl.when(band > 0)
        def _():
            og_ref[...] += grad.reshape(og_ref.shape)

        proj = dot(ctx, ow[...]).astype(BF16)
        back = dot(perm, proj, ((0,), (0,))).astype(BF16)
        write_band(own_ref, give_ref, back, band, shift_h, core)
        return 0

    lax.fori_loop(0, BANDS, body, 0)
    parts, rows, _ = og_out.shape

    def order(i, _):
        owner = lax.rem(shifts[3] + i, parts)
        og_out[i] = og_ref[owner].astype(BF16)
        return 0

    lax.fori_loop(0, parts, order, 0)


def backward_kernel(shifts, packed_ref, prob_ref, dctx_ref, w_ref, own_ref, give_ref, table_ref, dpk):
    shift_h = shifts[0]
    shift_w = shifts[1]
    perm = band_permutation(shift_w)
    scale = HD**-0.5
    table_ref[...] = jnp.zeros_like(table_ref)

    def body(band, _):
        for pair in range(2):
            rows = pl.ds(pl.multiple_of(band * BAND + pair * PAIR, PAIR), PAIR)
            packed = packed_ref[rows, :]
            dctx = dctx_ref[rows, :]
            dqs, dks, dvs = [], [], []
            for h in range(MINE):
                q = packed[:, h * HD : (h + 1) * HD]
                k = packed[:, HALF + h * HD : HALF + (h + 1) * HD]
                v = packed[:, 2 * HALF + h * HD : 2 * HALF + (h + 1) * HD]
                d = dctx[:, h * HD : (h + 1) * HD]
                p = prob_ref[(band * 2 + pair) * MINE + h]
                dp = dot(d, v, ((1,), (1,)))
                dvs.append(dot(p.astype(BF16), d, ((0,), (0,))).astype(BF16))
                ds = p * (dp - jnp.sum(p * dp, axis=-1, keepdims=True))
                table_ref[h] += ds
                low = ds.astype(BF16)
                dqs.append((dot(low, k) * scale).astype(BF16))
                dks.append((dot(low, q, ((0,), (0,))) * scale).astype(BF16))
            dpk[pair * PAIR : (pair + 1) * PAIR, :] = jnp.concatenate(dqs + dks + dvs, axis=1)
        dsh = dot(dpk[...], w_ref[...], ((1,), (1,))).astype(BF16)
        back = dot(perm, dsh, ((0,), (0,))).astype(BF16)
        write_band(own_ref, give_ref, back, band, shift_h, shifts[2])
        return 0

    lax.fori_loop(0, BANDS, body, 0)


def norm_kernel(x_ref, o_ref):
    values = x_ref[...].astype(F32)
    centered = values - jnp.mean(values, axis=-1, keepdims=True)
    scale = lax.rsqrt(jnp.mean(centered * centered, axis=-1, keepdims=True) + 1e-05)
    o_ref[...] = (centered * scale).astype(BF16)


def norm_back_kernel(x_ref, a_ref, b_ref, o_ref):
    values = x_ref[...].astype(F32)
    centered = values - jnp.mean(values, axis=-1, keepdims=True)
    scale = lax.rsqrt(jnp.mean(centered * centered, axis=-1, keepdims=True) + 1e-05)
    xhat = centered * scale
    grad = a_ref[...].astype(F32) + b_ref[...].astype(F32)
    grad = grad.astype(BF16).astype(F32)
    mean_grad = jnp.mean(grad, axis=-1, keepdims=True)
    mean_cross = jnp.mean(grad * xhat, axis=-1, keepdims=True)
    o_ref[...] = (scale * (grad - mean_grad - xhat * mean_cross)).astype(BF16)


def rowwise(kernel, *arrays):
    rows, cols, width = arrays[0].shape
    step = 4
    spec = pl.BlockSpec((step, cols, width), lambda i: (i, 0, 0))
    return pl.pallas_call(
        kernel,
        out_shape=jax.ShapeDtypeStruct(arrays[0].shape, BF16),
        grid=(rows // step,),
        in_specs=[spec] * len(arrays),
        out_specs=spec,
        cost_estimate=pl.CostEstimate(
            flops=20 * rows * cols * width, bytes_accessed=2 * rows * cols * width * 3, transcendentals=0
        ),
    )(*arrays)


def whole(count):
    return [pl.BlockSpec(memory_space=pltpu.VMEM)] * count


def shape(dims, kind):
    return jax.ShapeDtypeStruct(dims, kind)


def offset_table(window):
    span = 2 * window - 1
    position = jnp.arange(window, dtype=jnp.int32)
    offset = position[:, None] - position[None, :] + window - 1
    return (offset[:, :, None] == jnp.arange(span, dtype=jnp.int32)[None, None, :]).astype(F32)


def both_halves(own, other, core):
    return jnp.where(
        core == 0, jnp.concatenate([own, other], axis=0), jnp.concatenate([other, own], axis=0)
    )


MESH = pl.DeviceIdType.MESH


def ring_place(chip):
    z = chip // 2
    return jnp.where(chip % 2 == 0, z, 7 - z)


def ring_chip(place):
    place = (place + 8) % 8
    return jnp.where(place < 4, 2 * place, 2 * (7 - place) + 1)


def gather_kernel(
    w_ref, ow_ref, x_ref, cot_ref, w_out, ow_out, x_out, cot_out, normed,
    tok_send, tok_recv, local, pair_send, pair_recv, ring_send, ring_recv, cross_send, cross_recv,
):
    me = lax.axis_index("fsdp")
    group = lax.axis_index("groups")
    core = me % 2
    chip = me // 2
    place = ring_place(chip)
    right = ring_chip(place + 1) * 2 + core
    left = ring_chip(place - 1) * 2 + core
    other = chip * 2 + (1 - core)

    barrier = pltpu.get_barrier_semaphore()
    for target in ({"fsdp": other}, {"fsdp": right}, {"fsdp": left}, {"groups": 1 - group}):
        pl.semaphore_signal(barrier, inc=1, device_id=target, device_id_type=MESH)
    pl.semaphore_wait(barrier, 4)

    def remote(src, dst, send, recv, target):
        return pltpu.make_async_remote_copy(
            src_ref=src, dst_ref=dst, send_sem=send, recv_sem=recv, device_id=target, device_id_type=MESH
        )

    rows = w_ref.shape[0]
    own_rows = pl.ds(pl.multiple_of((chip * 2 + core) * rows, rows), rows)
    pairs, locals_ = [], []
    for kind in range(3):
        dst = w_out.at[own_rows, pl.ds(kind * HALF, HALF)]

        def columns(which):
            return w_ref.at[:, pl.ds(pl.multiple_of(kind * 2 * HALF + which * HALF, HALF), HALF)]

        pairs.append(
            remote(columns(1 - core), dst, pair_send.at[kind], pair_recv.at[kind], {"fsdp": other})
        )
        locals_.append(pltpu.make_async_copy(columns(core), dst, local.at[kind]))
    locals_.append(pltpu.make_async_copy(ow_ref, ow_out.at[chip, core], local.at[3]))
    for copy in pairs + locals_:
        copy.start()
    cot_far = remote(cot_ref, cot_out.at[core], tok_send.at[0], tok_recv.at[0], {"fsdp": other})
    cot_near = pltpu.make_async_copy(cot_ref, cot_out.at[core], local.at[4])
    for copy in locals_:
        copy.wait()
    for copy in pairs:
        copy.wait()

    third = 2 * rows // 3
    thin = ow_ref.shape[0] // 3

    def piece(name, chunk):
        part = group if name[1] == "m" else 2
        if name[0] == "w":
            start = pl.multiple_of(chunk * (2 * rows) + part * third, third)
            return w_out.at[pl.ds(start, third), :]
        return ow_out.at[chunk, core, pl.ds(pl.multiple_of(part * thin, thin), thin), :]

    names = ("wm", "wc", "om", "oc")

    def carried(way, step):
        if step < 4:
            return names
        return ("wm", "om") if way == 0 else ("wc", "oc")

    def hop(way, step, name):
        chunk = ring_chip(place - (step - 1) if way == 0 else place + (step - 1))
        ref = piece(name, chunk)
        i = names.index(name)
        return remote(
            ref, ref, ring_send.at[way, step - 1, i], ring_recv.at[way, step - 1, i],
            {"fsdp": right if way == 0 else left},
        )

    def arrival(way, step, name):
        chunk = ring_chip(place - step if way == 0 else place + step)
        ref = piece(name, chunk)
        i = names.index(name)
        return remote(
            ref, ref, ring_send.at[way, step - 1, i], ring_recv.at[way, step - 1, i],
            {"fsdp": right if way == 0 else left},
        )

    def cross(way, step, name, mine):
        chunk = ring_chip(place - step if way == 0 else place + step)
        part = group if mine else 1 - group
        if name == "wm":
            start = pl.multiple_of(chunk * (2 * rows) + part * third, third)
            ref = w_out.at[pl.ds(start, third), :]
        else:
            ref = ow_out.at[chunk, core, pl.ds(pl.multiple_of(part * thin, thin), thin), :]
        i = 0 if name == "wm" else 1
        return remote(
            ref, ref, cross_send.at[way, step - 1, i], cross_recv.at[way, step - 1, i],
            {"groups": 1 - group},
        )

    for name in names:
        for way in range(2):
            hop(way, 1, name).start()
    cot_far.start()
    cot_near.start()

    def norm_row(i, _):
        values = x_ref[i].astype(F32)
        centered = values - jnp.mean(values, axis=-1, keepdims=True)
        scale = lax.rsqrt(jnp.mean(centered * centered, axis=-1, keepdims=True) + 1e-05)
        normed[i] = (centered * scale).astype(BF16)
        return 0

    lax.fori_loop(0, x_ref.shape[0], norm_row, 0)
    x_far = remote(normed, x_out.at[core], tok_send.at[1], tok_recv.at[1], {"fsdp": other})
    x_near = pltpu.make_async_copy(normed, x_out.at[core], local.at[5])
    x_far.start()
    x_near.start()

    crossed = []
    for step in range(1, 5):
        for name in names:
            for way in range(2):
                if name not in carried(way, step):
                    continue
                arrival(way, step, name).wait_recv()
                if step < 4 and name in carried(way, step + 1):
                    hop(way, step + 1, name).start()
                if name[1] == "m":
                    cross(way, step, name, True).start()
                    crossed.append((way, step, name))
    for way, step, name in crossed:
        cross(way, step, name, False).wait_recv()
    half = ow_out.shape[0] // 2
    give = ow_out.at[pl.ds((1 - core) * half, half), core]
    swap = remote(give, give, pair_send.at[3], pair_recv.at[3], {"fsdp": other})
    swap.start()
    for step in range(1, 5):
        for way in range(2):
            for name in carried(way, step):
                hop(way, step, name).wait_send()
    for way, step, name in crossed:
        cross(way, step, name, True).wait_send()
    cot_far.wait()
    cot_near.wait()
    x_far.wait()
    x_near.wait()
    swap.wait()


def gathered(fields, in_weight, out_weight, cotangent):
    row_count, col_count, width = fields.shape
    count = lax.axis_size("fsdp")
    anywhere = pl.BlockSpec(memory_space=pl.ANY)
    dma = pltpu.SemaphoreType.DMA
    return pl.pallas_call(
        gather_kernel,
        out_shape=(
            shape((width, 3 * HALF), BF16),
            shape((count // 2, 2, out_weight.shape[0], width), BF16),
            shape((2, row_count, col_count, width), BF16),
            shape((2, row_count, col_count, width), BF16),
        ),
        in_specs=[anywhere, anywhere, pl.BlockSpec(memory_space=pltpu.VMEM), anywhere],
        out_specs=(anywhere,) * 4,
        scratch_shapes=[
            pltpu.VMEM(fields.shape, BF16),
            dma((2,)), dma((2,)), dma((6,)), dma((4,)), dma((4,)),
            dma((2, 4, 4)), dma((2, 4, 4)), dma((2, 4, 2)), dma((2, 4, 2)),
        ],
        compiler_params=pltpu.CompilerParams(
            collective_id=0, has_side_effects=True, vmem_limit_bytes=56 * 1024 * 1024
        ),
        cost_estimate=pl.CostEstimate(flops=10**8, bytes_accessed=10**8, transcendentals=0),
    )(in_weight, out_weight, fields, cotangent)


def gathered_plain(fields, in_weight, out_weight, cotangent):
    core = lax.axis_index("fsdp") % 2
    groups = same_core_groups()
    split = in_weight.reshape(in_weight.shape[0], 3, 2, HALF)
    keep = lax.dynamic_index_in_dim(split, core, 2, False).reshape(-1, 3 * HALF)
    give = lax.dynamic_index_in_dim(split, 1 - core, 2, False).reshape(-1, 3 * HALF)
    w_chip = both_halves(keep, partner(give), core)
    w_full = lax.all_gather(w_chip, "fsdp", axis=0, tiled=True, axis_index_groups=groups)
    ow_all = lax.all_gather(out_weight, "fsdp", axis=0, tiled=True)
    normed = rowwise(norm_kernel, fields)
    x_all = both_halves(normed, partner(normed), core)
    cot_all = both_halves(cotangent, partner(cotangent), core)
    return w_full, ow_all, x_all, cot_all


def shards(fields, shifts, in_weight, out_weight, bias_table, cotangent):
    row_count, col_count, width = fields.shape
    core = lax.axis_index("fsdp") % 2
    chips = lax.axis_size("fsdp") // 2
    span = 2 * WIN - 1
    area = WIN * WIN

    gather = gathered if 2 * chips == 16 else gathered_plain
    w_full, ow_all, x_all, cot_all = gather(fields, in_weight, out_weight, cotangent)
    ow_full = ow_all.reshape(2 * HALF, width)
    x_all = x_all.reshape(SIDE, col_count, width)
    cot_all = cot_all.reshape(SIDE, col_count, width)
    scalars = jnp.concatenate([shifts, jnp.stack([core, lax.axis_index("fsdp") // 2])]).astype(jnp.int32)

    table = offset_table(WIN)
    own_table = lax.dynamic_slice_in_dim(bias_table, core * MINE, MINE, 0)
    bias = jnp.einsum(
        "huv,pqu,rsv->hprqs",
        own_table.reshape(MINE, span, span),
        table,
        table,
        precision=lax.Precision.HIGHEST,
    ).reshape(MINE, area, area)
    bias = jnp.tile(bias, (1, 2, 2))

    tokens = SIDE * SIDE
    blocks = BANDS * 2 * MINE
    params = pltpu.CompilerParams(vmem_limit_bytes=VMEM_LIMIT)
    smem = pl.BlockSpec(memory_space=pltpu.SMEM)
    packed, prob, dctx, a_own, a_give, og = pl.pallas_call(
        forward_kernel,
        out_shape=(
            shape((tokens, 3 * HALF), BF16),
            shape((blocks, PAIR, PAIR), F32),
            shape((tokens, HALF), BF16),
            shape(fields.shape, BF16),
            shape(fields.shape, BF16),
            shape((chips, HALF // chips, width), BF16),
        ),
        in_specs=[smem] + whole(5),
        out_specs=tuple(whole(6)),
        scratch_shapes=[pltpu.VMEM((chips, HALF // chips, width), F32)],
        compiler_params=params,
        cost_estimate=pl.CostEstimate(flops=10**10, bytes_accessed=2 * 10**7, transcendentals=10**6),
    )(scalars, x_all, cot_all, w_full, ow_full, bias)

    terms = []
    for far in range(chips):
        route = [
            (2 * c + k, k * chips + (c + far) % chips) for c in range(chips) for k in range(2)
        ]
        terms.append(lax.ppermute(og[far], "fsdp", route))
    a_got = partner(a_give)

    d_own, d_give, score = pl.pallas_call(
        backward_kernel,
        out_shape=(
            shape(fields.shape, BF16),
            shape(fields.shape, BF16),
            shape((MINE, PAIR, PAIR), F32),
        ),
        in_specs=[smem] + whole(4),
        out_specs=tuple(whole(3)),
        scratch_shapes=[pltpu.VMEM((BAND, 3 * HALF), BF16)],
        compiler_params=params,
        cost_estimate=pl.CostEstimate(flops=10**10, bytes_accessed=2 * 10**7, transcendentals=10**6),
    )(scalars, packed, prob, dctx, w_full)

    d_got = partner(d_give)
    attended = (a_own.astype(F32) + a_got.astype(F32)).astype(BF16)
    fields_gradient = rowwise(norm_back_kernel, fields, d_own, d_got)
    out_grad = functools.reduce(jnp.add, [term.astype(F32) for term in terms])

    local = (score[:, :area, :area] + score[:, area:, area:]).reshape(MINE, WIN, WIN, WIN, WIN)
    own_grad = jnp.einsum(
        "hprqs,pqu,rsv->huv", local, table, table, precision=lax.Precision.HIGHEST
    ).reshape(MINE, span * span)
    padded = lax.dynamic_update_slice_in_dim(
        jnp.zeros((HEADS, span * span), F32), own_grad, core * MINE, 0
    )
    table_grad = padded
    count, stride = 2 * chips, 1
    while stride < count:
        route = [(d, d ^ stride) for d in range(count)]
        table_grad = table_grad + lax.ppermute(table_grad, "fsdp", route)
        stride *= 2
    return (attended, fields_gradient, out_grad, table_grad)


def solution(mesh):
    in_specs = (
        P(("groups", "fsdp"), None, None),
        P(),
        P("fsdp", None),
        P("fsdp", None),
        P(),
        P(("groups", "fsdp"), None, None),
    )
    out_specs = (
        P(("groups", "fsdp"), None, None),
        P(("groups", "fsdp"), None, None),
        P(("groups", "fsdp"), None),
        P("groups", None),
    )
    return jax.shard_map(shards, mesh=mesh, in_specs=in_specs, out_specs=out_specs, check_vma=False)
```

```python
import functools

import jax
import jax.numpy as jnp
from jax import lax
from jax.experimental import pallas as pl
from jax.experimental.pallas import tpu as pltpu
from jax.sharding import PartitionSpec as P

HEADS = 12
HD = 64
WIN = 8
SIDE = 32
MINE = HEADS // 2
HALF = MINE * HD
BAND = WIN * SIDE
PAIR = 2 * WIN * WIN
BANDS = SIDE // WIN
VMEM_LIMIT = 60 * 1024 * 1024
F32 = jnp.float32
BF16 = jnp.bfloat16


def dot(a, b, dims=((1,), (0,))):
    return lax.dot_general(a, b, (dims, ((), ())), preferred_element_type=F32)


def partner(block):
    count = lax.axis_size("fsdp")
    return lax.ppermute(block, "fsdp", [(d, d ^ 1) for d in range(count)])


def same_core_groups():
    count = lax.axis_size("fsdp")
    return [list(range(0, count, 2)), list(range(1, count, 2))]


def band_permutation(shift_w):
    t = lax.broadcasted_iota(jnp.int32, (BAND, BAND), 0)
    s = lax.broadcasted_iota(jnp.int32, (BAND, BAND), 1)
    row = (t >> 3) & 7
    col = ((t >> 6) * WIN + (t & 7) + shift_w) & (SIDE - 1)
    return (row * SIDE + col == s).astype(F32).astype(BF16)


def pair_labels(band, pair, shift_h, shift_w, axis):
    shape = (PAIR, 1) if axis == 0 else (1, PAIR)
    t = lax.broadcasted_iota(jnp.int32, shape, axis)
    which = t >> 6
    row = band * WIN + ((t >> 3) & 7)
    col = pair * 2 * WIN + which * WIN + (t & 7)

    def label(index, shift):
        return jnp.where(index >= SIDE - WIN, 1, 0) + jnp.where(index >= SIDE - shift, 1, 0)

    return which * 16 + 3 * label(row, shift_h) + label(col, shift_w)


def read_band(ref, band, shift_h):
    rows = [ref[(band * WIN + i + shift_h) & (SIDE - 1)] for i in range(WIN)]
    return jnp.concatenate(rows, axis=0)


def write_band(own_ref, give_ref, value, band, shift_h, core):
    half = SIDE // 2
    for i in range(WIN):
        row = (band * WIN + i + shift_h) & (SIDE - 1)
        inside = row & (half - 1)
        mine = row // half == core

        @pl.when(mine)
        def _():
            own_ref[inside] = value[i * SIDE : (i + 1) * SIDE]

        @pl.when(jnp.logical_not(mine))
        def _():
            give_ref[inside] = value[i * SIDE : (i + 1) * SIDE]


def forward_kernel(
    shifts, x_ref, cot_ref, w_ref, ow_ref, bias_ref, packed_ref, prob_ref, dctx_ref, own_ref, give_ref, og_out, og_ref
):
    shift_h = shifts[0]
    shift_w = shifts[1]
    core = shifts[2]
    perm = band_permutation(shift_w)
    ow = ow_ref.at[pl.ds(pl.multiple_of(core * HALF, HALF), HALF), :]

    def body(band, _):
        tokens = pl.ds(pl.multiple_of(band * BAND, BAND), BAND)
        xs = dot(perm, read_band(x_ref, band, shift_h)).astype(BF16)
        packed = dot(xs, w_ref[...]).astype(BF16)
        packed_ref[tokens, :] = packed
        cot = dot(perm, read_band(cot_ref, band, shift_h)).astype(BF16)
        dctx_ref[tokens, :] = dot(cot, ow[...], ((1,), (1,))).astype(BF16)
        pairs = []
        for pair in range(2):
            rows = slice(pair * PAIR, (pair + 1) * PAIR)
            allowed = pair_labels(band, pair, shift_h, shift_w, 0) == pair_labels(
                band, pair, shift_h, shift_w, 1
            )
            heads = []
            for h in range(MINE):
                q = packed[rows, h * HD : (h + 1) * HD]
                k = packed[rows, HALF + h * HD : HALF + (h + 1) * HD]
                v = packed[rows, 2 * HALF + h * HD : 2 * HALF + (h + 1) * HD]
                s = dot(q, k, ((1,), (1,))) * (HD**-0.5) + bias_ref[h]
                s = jnp.where(allowed, s, -1e9)
                e = jnp.exp(s - jnp.max(s, axis=-1, keepdims=True))
                p = e / jnp.sum(e, axis=-1, keepdims=True)
                prob_ref[(band * 2 + pair) * MINE + h] = p
                heads.append(dot(p.astype(BF16), v).astype(BF16))
            pairs.append(jnp.concatenate(heads, axis=1))
        ctx = jnp.concatenate(pairs, axis=0)
        grad = dot(ctx, cot, ((0,), (0,)))

        @pl.when(band == 0)
        def _():
            og_ref[...] = grad.reshape(og_ref.shape)

        @pl.when(band > 0)
        def _():
            og_ref[...] += grad.reshape(og_ref.shape)

        proj = dot(ctx, ow[...]).astype(BF16)
        back = dot(perm, proj, ((0,), (0,))).astype(BF16)
        write_band(own_ref, give_ref, back, band, shift_h, core)
        return 0

    lax.fori_loop(0, BANDS, body, 0)
    parts, rows, _ = og_out.shape

    def order(i, _):
        owner = lax.rem(shifts[3] + i, parts)
        og_out[i] = og_ref[owner].astype(BF16)
        return 0

    lax.fori_loop(0, parts, order, 0)


def backward_kernel(shifts, packed_ref, prob_ref, dctx_ref, w_ref, own_ref, give_ref, table_ref, dpk):
    shift_h = shifts[0]
    shift_w = shifts[1]
    perm = band_permutation(shift_w)
    scale = HD**-0.5
    table_ref[...] = jnp.zeros_like(table_ref)

    def body(band, _):
        for pair in range(2):
            rows = pl.ds(pl.multiple_of(band * BAND + pair * PAIR, PAIR), PAIR)
            packed = packed_ref[rows, :]
            dctx = dctx_ref[rows, :]
            dqs, dks, dvs = [], [], []
            for h in range(MINE):
                q = packed[:, h * HD : (h + 1) * HD]
                k = packed[:, HALF + h * HD : HALF + (h + 1) * HD]
                v = packed[:, 2 * HALF + h * HD : 2 * HALF + (h + 1) * HD]
                d = dctx[:, h * HD : (h + 1) * HD]
                p = prob_ref[(band * 2 + pair) * MINE + h]
                dp = dot(d, v, ((1,), (1,)))
                dvs.append(dot(p.astype(BF16), d, ((0,), (0,))).astype(BF16))
                ds = p * (dp - jnp.sum(p * dp, axis=-1, keepdims=True))
                table_ref[h] += ds
                low = ds.astype(BF16)
                dqs.append((dot(low, k) * scale).astype(BF16))
                dks.append((dot(low, q, ((0,), (0,))) * scale).astype(BF16))
            dpk[pair * PAIR : (pair + 1) * PAIR, :] = jnp.concatenate(dqs + dks + dvs, axis=1)
        dsh = dot(dpk[...], w_ref[...], ((1,), (1,))).astype(BF16)
        back = dot(perm, dsh, ((0,), (0,))).astype(BF16)
        write_band(own_ref, give_ref, back, band, shift_h, shifts[2])
        return 0

    lax.fori_loop(0, BANDS, body, 0)


def joint_kernel(
    shifts, packed_ref, prob_ref, dctx_ref, w_ref, og_ref, give_ref,
    down_ref, dgot_ref, agot_ref, out_ref, score_ref,
    dpk, table, first, second, slots, sums, seen,
    part_send, part_recv, local, tok_send, tok_recv, cube_send, cube_recv,
):
    me = lax.axis_index("fsdp")
    core = me % 2
    chip = me // 2
    count = 16
    other = chip * 2 + (1 - core)
    barrier = pltpu.get_barrier_semaphore()
    for far in range(1, count):
        pl.semaphore_signal(
            barrier, inc=1, device_id={"fsdp": (me + far) % count}, device_id_type=MESH
        )
    pl.semaphore_wait(barrier, count - 1)

    def remote(src, dst, send, recv, target):
        return pltpu.make_async_remote_copy(
            src_ref=src, dst_ref=dst, send_sem=send, recv_sem=recv,
            device_id={"fsdp": target}, device_id_type=MESH,
        )

    a_copy = remote(give_ref, agot_ref, tok_send.at[0], tok_recv.at[0], other)
    a_copy.start()
    dests = [core * 8 + (chip + far) % 8 for far in range(8)]

    def part(far):
        return remote(
            og_ref.at[far], slots.at[far], part_send.at[far], part_recv.at[far], dests[far]
        )

    def near(far):
        return pltpu.make_async_copy(og_ref.at[far], slots.at[far], local.at[far])

    for far in range(8):

        @pl.when(dests[far] != me)
        def _():
            part(far).start()

        @pl.when(dests[far] == me)
        def _():
            near(far).start()

    backward_bands(shifts, packed_ref, prob_ref, dctx_ref, w_ref, first, table, dpk)

    sums[0] = table[:, :64, :64] + table[:, 64:, 64:]

    def cube(step):
        peer = chip + (1 << step) * (1 - 2 * ((chip // (1 << step)) % 2))
        return remote(
            sums.at[step], seen.at[step], cube_send.at[step], cube_recv.at[step], peer * 2 + core
        )

    src, dst = first, second
    for step in range(3):
        cube(step).start()
        taken = (shifts[0] >> step) & 1
        back = 1 << step

        def roll(row, _):
            dst[row] = jnp.where(taken == 1, src[lax.rem(row + SIDE - back, SIDE)], src[row])
            return 0

        lax.fori_loop(0, SIDE, roll, 0)
        src, dst = dst, src
        if step == 2:
            half = SIDE // 2
            d_copy = remote(
                src.at[pl.ds((1 - core) * half, half)], dgot_ref, tok_send.at[1], tok_recv.at[1], other
            )
            d_copy.start()
        cube(step).wait()
        sums[step + 1] = sums[step] + seen[step]
    last = remote(sums.at[3], seen.at[3], cube_send.at[3], cube_recv.at[3], other)
    last.start()

    def keep(row, _):
        down_ref[row] = src[core * (SIDE // 2) + row]
        return 0

    lax.fori_loop(0, SIDE // 2, keep, 0)
    for far in range(8):

        @pl.when(dests[far] != me)
        def _():
            part(far).wait()

        @pl.when(dests[far] == me)
        def _():
            near(far).wait()

    total = slots[0].astype(F32)
    for far in range(1, 8):
        total = total + slots[far].astype(F32)
    out_ref[...] = total
    last.wait()
    score_ref[core] = sums[3]
    score_ref[1 - core] = seen[3]
    a_copy.wait()
    d_copy.wait()


def backward_bands(shifts, packed_ref, prob_ref, dctx_ref, w_ref, out_ref, table_ref, dpk):
    shift_w = shifts[1]
    perm = band_permutation(shift_w)
    scale = HD**-0.5
    table_ref[...] = jnp.zeros_like(table_ref)

    def body(band, _):
        for pair in range(2):
            rows = pl.ds(pl.multiple_of(band * BAND + pair * PAIR, PAIR), PAIR)
            packed = packed_ref[rows, :]
            dctx = dctx_ref[rows, :]
            dqs, dks, dvs = [], [], []
            for h in range(MINE):
                q = packed[:, h * HD : (h + 1) * HD]
                k = packed[:, HALF + h * HD : HALF + (h + 1) * HD]
                v = packed[:, 2 * HALF + h * HD : 2 * HALF + (h + 1) * HD]
                d = dctx[:, h * HD : (h + 1) * HD]
                p = prob_ref[(band * 2 + pair) * MINE + h]
                dp = dot(d, v, ((1,), (1,)))
                dvs.append(dot(p.astype(BF16), d, ((0,), (0,))).astype(BF16))
                ds = p * (dp - jnp.sum(p * dp, axis=-1, keepdims=True))
                table_ref[h] += ds
                low = ds.astype(BF16)
                dqs.append((dot(low, k) * scale).astype(BF16))
                dks.append((dot(low, q, ((0,), (0,))) * scale).astype(BF16))
            dpk[pair * PAIR : (pair + 1) * PAIR, :] = jnp.concatenate(dqs + dks + dvs, axis=1)
        dsh = dot(dpk[...], w_ref[...], ((1,), (1,))).astype(BF16)
        back = dot(perm, dsh, ((0,), (0,))).astype(BF16)
        for i in range(WIN):
            out_ref[band * WIN + i] = back[i * SIDE : (i + 1) * SIDE]
        return 0

    lax.fori_loop(0, BANDS, body, 0)


def norm_kernel(x_ref, o_ref):
    values = x_ref[...].astype(F32)
    centered = values - jnp.mean(values, axis=-1, keepdims=True)
    scale = lax.rsqrt(jnp.mean(centered * centered, axis=-1, keepdims=True) + 1e-05)
    o_ref[...] = (centered * scale).astype(BF16)


def norm_back_kernel(x_ref, a_ref, b_ref, o_ref):
    values = x_ref[...].astype(F32)
    centered = values - jnp.mean(values, axis=-1, keepdims=True)
    scale = lax.rsqrt(jnp.mean(centered * centered, axis=-1, keepdims=True) + 1e-05)
    xhat = centered * scale
    grad = a_ref[...].astype(F32) + b_ref[...].astype(F32)
    grad = grad.astype(BF16).astype(F32)
    mean_grad = jnp.mean(grad, axis=-1, keepdims=True)
    mean_cross = jnp.mean(grad * xhat, axis=-1, keepdims=True)
    o_ref[...] = (scale * (grad - mean_grad - xhat * mean_cross)).astype(BF16)


def rowwise(kernel, *arrays):
    rows, cols, width = arrays[0].shape
    step = 4
    spec = pl.BlockSpec((step, cols, width), lambda i: (i, 0, 0))
    return pl.pallas_call(
        kernel,
        out_shape=jax.ShapeDtypeStruct(arrays[0].shape, BF16),
        grid=(rows // step,),
        in_specs=[spec] * len(arrays),
        out_specs=spec,
        cost_estimate=pl.CostEstimate(
            flops=20 * rows * cols * width, bytes_accessed=2 * rows * cols * width * 3, transcendentals=0
        ),
    )(*arrays)


def whole(count):
    return [pl.BlockSpec(memory_space=pltpu.VMEM)] * count


def shape(dims, kind):
    return jax.ShapeDtypeStruct(dims, kind)


def offset_table(window):
    span = 2 * window - 1
    position = jnp.arange(window, dtype=jnp.int32)
    offset = position[:, None] - position[None, :] + window - 1
    return (offset[:, :, None] == jnp.arange(span, dtype=jnp.int32)[None, None, :]).astype(F32)


def both_halves(own, other, core):
    return jnp.where(
        core == 0, jnp.concatenate([own, other], axis=0), jnp.concatenate([other, own], axis=0)
    )


MESH = pl.DeviceIdType.MESH


def ring_place(chip):
    z = chip // 2
    return jnp.where(chip % 2 == 0, z, 7 - z)


def ring_chip(place):
    place = (place + 8) % 8
    return jnp.where(place < 4, 2 * place, 2 * (7 - place) + 1)


def gather_kernel(
    w_ref, ow_ref, x_ref, cot_ref, w_out, ow_out, x_out, cot_out, normed,
    tok_send, tok_recv, local, pair_send, pair_recv, ring_send, ring_recv, cross_send, cross_recv,
):
    me = lax.axis_index("fsdp")
    group = lax.axis_index("groups")
    core = me % 2
    chip = me // 2
    place = ring_place(chip)
    right = ring_chip(place + 1) * 2 + core
    left = ring_chip(place - 1) * 2 + core
    other = chip * 2 + (1 - core)

    barrier = pltpu.get_barrier_semaphore()
    for target in ({"fsdp": other}, {"fsdp": right}, {"fsdp": left}, {"groups": 1 - group}):
        pl.semaphore_signal(barrier, inc=1, device_id=target, device_id_type=MESH)
    pl.semaphore_wait(barrier, 4)

    def remote(src, dst, send, recv, target):
        return pltpu.make_async_remote_copy(
            src_ref=src, dst_ref=dst, send_sem=send, recv_sem=recv, device_id=target, device_id_type=MESH
        )

    rows = w_ref.shape[0]
    own_rows = pl.ds(pl.multiple_of((chip * 2 + core) * rows, rows), rows)
    pairs, locals_ = [], []
    for kind in range(3):
        dst = w_out.at[own_rows, pl.ds(kind * HALF, HALF)]

        def columns(which):
            return w_ref.at[:, pl.ds(pl.multiple_of(kind * 2 * HALF + which * HALF, HALF), HALF)]

        pairs.append(
            remote(columns(1 - core), dst, pair_send.at[kind], pair_recv.at[kind], {"fsdp": other})
        )
        locals_.append(pltpu.make_async_copy(columns(core), dst, local.at[kind]))
    locals_.append(pltpu.make_async_copy(ow_ref, ow_out.at[chip, core], local.at[3]))
    for copy in pairs + locals_:
        copy.start()
    cot_far = remote(cot_ref, cot_out.at[core], tok_send.at[0], tok_recv.at[0], {"fsdp": other})
    cot_near = pltpu.make_async_copy(cot_ref, cot_out.at[core], local.at[4])
    for copy in locals_:
        copy.wait()
    for copy in pairs:
        copy.wait()

    third = 2 * rows // 3
    thin = ow_ref.shape[0] // 3

    def piece(name, chunk):
        part = group if name[1] == "m" else 2
        if name[0] == "w":
            start = pl.multiple_of(chunk * (2 * rows) + part * third, third)
            return w_out.at[pl.ds(start, third), :]
        return ow_out.at[chunk, core, pl.ds(pl.multiple_of(part * thin, thin), thin), :]

    names = ("wm", "wc", "om", "oc")

    def carried(way, step):
        if step < 4:
            return names
        return ("wm", "om") if way == 0 else ("wc", "oc")

    def hop(way, step, name):
        chunk = ring_chip(place - (step - 1) if way == 0 else place + (step - 1))
        ref = piece(name, chunk)
        i = names.index(name)
        return remote(
            ref, ref, ring_send.at[way, step - 1, i], ring_recv.at[way, step - 1, i],
            {"fsdp": right if way == 0 else left},
        )

    def arrival(way, step, name):
        chunk = ring_chip(place - step if way == 0 else place + step)
        ref = piece(name, chunk)
        i = names.index(name)
        return remote(
            ref, ref, ring_send.at[way, step - 1, i], ring_recv.at[way, step - 1, i],
            {"fsdp": right if way == 0 else left},
        )

    def cross(way, step, name, mine):
        chunk = ring_chip(place - step if way == 0 else place + step)
        part = group if mine else 1 - group
        if name == "wm":
            start = pl.multiple_of(chunk * (2 * rows) + part * third, third)
            ref = w_out.at[pl.ds(start, third), :]
        else:
            ref = ow_out.at[chunk, core, pl.ds(pl.multiple_of(part * thin, thin), thin), :]
        i = 0 if name == "wm" else 1
        return remote(
            ref, ref, cross_send.at[way, step - 1, i], cross_recv.at[way, step - 1, i],
            {"groups": 1 - group},
        )

    for name in names:
        for way in range(2):
            hop(way, 1, name).start()
    cot_far.start()
    cot_near.start()

    def norm_row(i, _):
        values = x_ref[i].astype(F32)
        centered = values - jnp.mean(values, axis=-1, keepdims=True)
        scale = lax.rsqrt(jnp.mean(centered * centered, axis=-1, keepdims=True) + 1e-05)
        normed[i] = (centered * scale).astype(BF16)
        return 0

    lax.fori_loop(0, x_ref.shape[0], norm_row, 0)
    x_far = remote(normed, x_out.at[core], tok_send.at[1], tok_recv.at[1], {"fsdp": other})
    x_near = pltpu.make_async_copy(normed, x_out.at[core], local.at[5])
    x_far.start()
    x_near.start()

    crossed = []
    for step in range(1, 5):
        for name in names:
            for way in range(2):
                if name not in carried(way, step):
                    continue
                arrival(way, step, name).wait_recv()
                if step < 4 and name in carried(way, step + 1):
                    hop(way, step + 1, name).start()
                if name[1] == "m":
                    cross(way, step, name, True).start()
                    crossed.append((way, step, name))
    for way, step, name in crossed:
        cross(way, step, name, False).wait_recv()
    half = ow_out.shape[0] // 2
    give = ow_out.at[pl.ds((1 - core) * half, half), core]
    swap = remote(give, give, pair_send.at[3], pair_recv.at[3], {"fsdp": other})
    swap.start()
    for step in range(1, 5):
        for way in range(2):
            for name in carried(way, step):
                hop(way, step, name).wait_send()
    for way, step, name in crossed:
        cross(way, step, name, True).wait_send()
    cot_far.wait()
    cot_near.wait()
    x_far.wait()
    x_near.wait()
    swap.wait()


def gathered(fields, in_weight, out_weight, cotangent):
    row_count, col_count, width = fields.shape
    count = lax.axis_size("fsdp")
    anywhere = pl.BlockSpec(memory_space=pl.ANY)
    dma = pltpu.SemaphoreType.DMA
    return pl.pallas_call(
        gather_kernel,
        out_shape=(
            shape((width, 3 * HALF), BF16),
            shape((count // 2, 2, out_weight.shape[0], width), BF16),
            shape((2, row_count, col_count, width), BF16),
            shape((2, row_count, col_count, width), BF16),
        ),
        in_specs=[anywhere, anywhere, pl.BlockSpec(memory_space=pltpu.VMEM), anywhere],
        out_specs=(anywhere,) * 4,
        scratch_shapes=[
            pltpu.VMEM(fields.shape, BF16),
            dma((2,)), dma((2,)), dma((6,)), dma((4,)), dma((4,)),
            dma((2, 4, 4)), dma((2, 4, 4)), dma((2, 4, 2)), dma((2, 4, 2)),
        ],
        compiler_params=pltpu.CompilerParams(
            collective_id=0, has_side_effects=True, vmem_limit_bytes=56 * 1024 * 1024
        ),
        cost_estimate=pl.CostEstimate(flops=10**8, bytes_accessed=10**8, transcendentals=0),
    )(in_weight, out_weight, fields, cotangent)


def joint_call(scalars, packed, prob, dctx, w_full, og, give):
    dma = pltpu.SemaphoreType.DMA
    area = WIN * WIN
    return pl.pallas_call(
        joint_kernel,
        out_shape=(
            shape(give.shape, BF16),
            shape(give.shape, BF16),
            shape(give.shape, BF16),
            shape(og.shape[1:], F32),
            shape((2, MINE, area, area), F32),
        ),
        in_specs=[pl.BlockSpec(memory_space=pltpu.SMEM)] + whole(6),
        out_specs=tuple(whole(5)),
        scratch_shapes=[
            pltpu.VMEM((BAND, 3 * HALF), BF16),
            pltpu.VMEM((MINE, PAIR, PAIR), F32),
            pltpu.VMEM((SIDE, SIDE, give.shape[2]), BF16),
            pltpu.VMEM((SIDE, SIDE, give.shape[2]), BF16),
            pltpu.VMEM(og.shape, BF16),
            pltpu.VMEM((4, MINE, area, area), F32),
            pltpu.VMEM((4, MINE, area, area), F32),
            dma((8,)), dma((8,)), dma((8,)), dma((2,)), dma((2,)), dma((4,)), dma((4,)),
        ],
        compiler_params=pltpu.CompilerParams(
            collective_id=1, has_side_effects=True, vmem_limit_bytes=VMEM_LIMIT
        ),
        cost_estimate=pl.CostEstimate(flops=10**10, bytes_accessed=2 * 10**7, transcendentals=0),
    )(scalars, packed, prob, dctx, w_full, og, give)


def gathered_plain(fields, in_weight, out_weight, cotangent):
    core = lax.axis_index("fsdp") % 2
    groups = same_core_groups()
    split = in_weight.reshape(in_weight.shape[0], 3, 2, HALF)
    keep = lax.dynamic_index_in_dim(split, core, 2, False).reshape(-1, 3 * HALF)
    give = lax.dynamic_index_in_dim(split, 1 - core, 2, False).reshape(-1, 3 * HALF)
    w_chip = both_halves(keep, partner(give), core)
    w_full = lax.all_gather(w_chip, "fsdp", axis=0, tiled=True, axis_index_groups=groups)
    ow_all = lax.all_gather(out_weight, "fsdp", axis=0, tiled=True)
    normed = rowwise(norm_kernel, fields)
    x_all = both_halves(normed, partner(normed), core)
    cot_all = both_halves(cotangent, partner(cotangent), core)
    return w_full, ow_all, x_all, cot_all


def shards(fields, shifts, in_weight, out_weight, bias_table, cotangent):
    row_count, col_count, width = fields.shape
    core = lax.axis_index("fsdp") % 2
    chips = lax.axis_size("fsdp") // 2
    span = 2 * WIN - 1
    area = WIN * WIN

    gather = gathered if 2 * chips == 16 else gathered_plain
    w_full, ow_all, x_all, cot_all = gather(fields, in_weight, out_weight, cotangent)
    ow_full = ow_all.reshape(2 * HALF, width)
    x_all = x_all.reshape(SIDE, col_count, width)
    cot_all = cot_all.reshape(SIDE, col_count, width)
    scalars = jnp.concatenate([shifts, jnp.stack([core, lax.axis_index("fsdp") // 2])]).astype(jnp.int32)

    table = offset_table(WIN)
    own_table = lax.dynamic_slice_in_dim(bias_table, core * MINE, MINE, 0)
    bias = jnp.einsum(
        "huv,pqu,rsv->hprqs",
        own_table.reshape(MINE, span, span),
        table,
        table,
        precision=lax.Precision.HIGHEST,
    ).reshape(MINE, area, area)
    bias = jnp.tile(bias, (1, 2, 2))

    tokens = SIDE * SIDE
    blocks = BANDS * 2 * MINE
    params = pltpu.CompilerParams(vmem_limit_bytes=VMEM_LIMIT)
    smem = pl.BlockSpec(memory_space=pltpu.SMEM)
    packed, prob, dctx, a_own, a_give, og = pl.pallas_call(
        forward_kernel,
        out_shape=(
            shape((tokens, 3 * HALF), BF16),
            shape((blocks, PAIR, PAIR), F32),
            shape((tokens, HALF), BF16),
            shape(fields.shape, BF16),
            shape(fields.shape, BF16),
            shape((chips, HALF // chips, width), BF16),
        ),
        in_specs=[smem] + whole(5),
        out_specs=tuple(whole(6)),
        scratch_shapes=[pltpu.VMEM((chips, HALF // chips, width), F32)],
        compiler_params=params,
        cost_estimate=pl.CostEstimate(flops=10**10, bytes_accessed=2 * 10**7, transcendentals=10**6),
    )(scalars, x_all, cot_all, w_full, ow_full, bias)

    joint = 2 * chips == 16
    terms = []
    for far in range(0 if joint else chips):
        route = [
            (2 * c + k, k * chips + (c + far) % chips) for c in range(chips) for k in range(2)
        ]
        terms.append(lax.ppermute(og[far], "fsdp", route))
    if joint:
        d_own, d_got, a_got, out_grad, score = joint_call(
            scalars, packed, prob, dctx, w_full, og, a_give
        )
        attended = (a_own.astype(F32) + a_got.astype(F32)).astype(BF16)
        fields_gradient = rowwise(norm_back_kernel, fields, d_own, d_got)
        local = score.reshape(HEADS, WIN, WIN, WIN, WIN)
        table_grad = jnp.einsum(
            "hprqs,pqu,rsv->huv", local, table, table, precision=lax.Precision.HIGHEST
        ).reshape(HEADS, span * span)
        return (attended, fields_gradient, out_grad, table_grad)
    a_got = partner(a_give)

    d_own, d_give, score = pl.pallas_call(
        backward_kernel,
        out_shape=(
            shape(fields.shape, BF16),
            shape(fields.shape, BF16),
            shape((MINE, PAIR, PAIR), F32),
        ),
        in_specs=[smem] + whole(4),
        out_specs=tuple(whole(3)),
        scratch_shapes=[pltpu.VMEM((BAND, 3 * HALF), BF16)],
        compiler_params=params,
        cost_estimate=pl.CostEstimate(flops=10**10, bytes_accessed=2 * 10**7, transcendentals=10**6),
    )(scalars, packed, prob, dctx, w_full)

    d_got = partner(d_give)
    attended = (a_own.astype(F32) + a_got.astype(F32)).astype(BF16)
    fields_gradient = rowwise(norm_back_kernel, fields, d_own, d_got)
    out_grad = functools.reduce(jnp.add, [term.astype(F32) for term in terms])

    local = (score[:, :area, :area] + score[:, area:, area:]).reshape(MINE, WIN, WIN, WIN, WIN)
    own_grad = jnp.einsum(
        "hprqs,pqu,rsv->huv", local, table, table, precision=lax.Precision.HIGHEST
    ).reshape(MINE, span * span)
    padded = lax.dynamic_update_slice_in_dim(
        jnp.zeros((HEADS, span * span), F32), own_grad, core * MINE, 0
    )
    table_grad = padded
    count, stride = 2 * chips, 1
    while stride < count:
        route = [(d, d ^ stride) for d in range(count)]
        table_grad = table_grad + lax.ppermute(table_grad, "fsdp", route)
        stride *= 2
    return (attended, fields_gradient, out_grad, table_grad)


def solution(mesh):
    in_specs = (
        P(("groups", "fsdp"), None, None),
        P(),
        P("fsdp", None),
        P("fsdp", None),
        P(),
        P(("groups", "fsdp"), None, None),
    )
    out_specs = (
        P(("groups", "fsdp"), None, None),
        P(("groups", "fsdp"), None, None),
        P(("groups", "fsdp"), None),
        P("groups", None),
    )
    return jax.shard_map(shards, mesh=mesh, in_specs=in_specs, out_specs=out_specs, check_vma=False)
```

```python
import functools

import jax
import jax.numpy as jnp
from jax import lax
from jax.experimental import pallas as pl
from jax.experimental.pallas import tpu as pltpu
from jax.sharding import PartitionSpec as P

HEADS = 12
HD = 64
WIN = 8
SIDE = 32
MINE = HEADS // 2
HALF = MINE * HD
BAND = WIN * SIDE
PAIR = 2 * WIN * WIN
BANDS = SIDE // WIN
VMEM_LIMIT = 60 * 1024 * 1024
F32 = jnp.float32
BF16 = jnp.bfloat16


def dot(a, b, dims=((1,), (0,))):
    return lax.dot_general(a, b, (dims, ((), ())), preferred_element_type=F32)


def partner(block):
    count = lax.axis_size("fsdp")
    return lax.ppermute(block, "fsdp", [(d, d ^ 1) for d in range(count)])


def same_core_groups():
    count = lax.axis_size("fsdp")
    return [list(range(0, count, 2)), list(range(1, count, 2))]


def band_permutation(shift_w):
    t = lax.broadcasted_iota(jnp.int32, (BAND, BAND), 0)
    s = lax.broadcasted_iota(jnp.int32, (BAND, BAND), 1)
    row = (t >> 3) & 7
    col = ((t >> 6) * WIN + (t & 7) + shift_w) & (SIDE - 1)
    return (row * SIDE + col == s).astype(F32).astype(BF16)


def pair_labels(band, pair, shift_h, shift_w, axis):
    shape = (PAIR, 1) if axis == 0 else (1, PAIR)
    t = lax.broadcasted_iota(jnp.int32, shape, axis)
    which = t >> 6
    row = band * WIN + ((t >> 3) & 7)
    col = pair * 2 * WIN + which * WIN + (t & 7)

    def label(index, shift):
        return jnp.where(index >= SIDE - WIN, 1, 0) + jnp.where(index >= SIDE - shift, 1, 0)

    return which * 16 + 3 * label(row, shift_h) + label(col, shift_w)


def read_band(ref, band, shift_h):
    rows = [ref[(band * WIN + i + shift_h) & (SIDE - 1)] for i in range(WIN)]
    return jnp.concatenate(rows, axis=0)


def write_band(own_ref, give_ref, value, band, shift_h, core):
    half = SIDE // 2
    for i in range(WIN):
        row = (band * WIN + i + shift_h) & (SIDE - 1)
        inside = row & (half - 1)
        mine = row // half == core

        @pl.when(mine)
        def _():
            own_ref[inside] = value[i * SIDE : (i + 1) * SIDE]

        @pl.when(jnp.logical_not(mine))
        def _():
            give_ref[inside] = value[i * SIDE : (i + 1) * SIDE]


def forward_kernel(
    shifts, x_ref, cot_ref, w_ref, ow_ref, bias_ref, packed_ref, prob_ref, dctx_ref, own_ref, give_ref, og_out, og_ref
):
    shift_h = shifts[0]
    shift_w = shifts[1]
    core = shifts[2]
    perm = band_permutation(shift_w)
    ow = ow_ref.at[pl.ds(pl.multiple_of(core * HALF, HALF), HALF), :]

    def body(band, _):
        tokens = pl.ds(pl.multiple_of(band * BAND, BAND), BAND)
        xs = dot(perm, read_band(x_ref, band, shift_h)).astype(BF16)
        packed = dot(xs, w_ref[...]).astype(BF16)
        packed_ref[tokens, :] = packed
        cot = dot(perm, read_band(cot_ref, band, shift_h)).astype(BF16)
        dctx_ref[tokens, :] = dot(cot, ow[...], ((1,), (1,))).astype(BF16)
        pairs = []
        for pair in range(2):
            rows = slice(pair * PAIR, (pair + 1) * PAIR)
            allowed = pair_labels(band, pair, shift_h, shift_w, 0) == pair_labels(
                band, pair, shift_h, shift_w, 1
            )
            heads = []
            for h in range(MINE):
                q = packed[rows, h * HD : (h + 1) * HD]
                k = packed[rows, HALF + h * HD : HALF + (h + 1) * HD]
                v = packed[rows, 2 * HALF + h * HD : 2 * HALF + (h + 1) * HD]
                s = dot(q, k, ((1,), (1,))) * (HD**-0.5) + bias_ref[h]
                s = jnp.where(allowed, s, -1e9)
                e = jnp.exp(s - jnp.max(s, axis=-1, keepdims=True))
                p = e / jnp.sum(e, axis=-1, keepdims=True)
                prob_ref[(band * 2 + pair) * MINE + h] = p
                heads.append(dot(p.astype(BF16), v).astype(BF16))
            pairs.append(jnp.concatenate(heads, axis=1))
        ctx = jnp.concatenate(pairs, axis=0)
        grad = dot(ctx, cot, ((0,), (0,)))

        @pl.when(band == 0)
        def _():
            og_ref[...] = grad.reshape(og_ref.shape)

        @pl.when(band > 0)
        def _():
            og_ref[...] += grad.reshape(og_ref.shape)

        proj = dot(ctx, ow[...]).astype(BF16)
        back = dot(perm, proj, ((0,), (0,))).astype(BF16)
        write_band(own_ref, give_ref, back, band, shift_h, core)
        return 0

    lax.fori_loop(0, BANDS, body, 0)
    parts, rows, _ = og_out.shape

    def order(i, _):
        owner = lax.rem(shifts[3] + i, parts)
        og_out[i] = og_ref[owner].astype(BF16)
        return 0

    lax.fori_loop(0, parts, order, 0)


def backward_kernel(shifts, packed_ref, prob_ref, dctx_ref, w_ref, own_ref, give_ref, table_ref, dpk):
    shift_h = shifts[0]
    shift_w = shifts[1]
    perm = band_permutation(shift_w)
    scale = HD**-0.5
    table_ref[...] = jnp.zeros_like(table_ref)

    def body(band, _):
        for pair in range(2):
            rows = pl.ds(pl.multiple_of(band * BAND + pair * PAIR, PAIR), PAIR)
            packed = packed_ref[rows, :]
            dctx = dctx_ref[rows, :]
            dqs, dks, dvs = [], [], []
            for h in range(MINE):
                q = packed[:, h * HD : (h + 1) * HD]
                k = packed[:, HALF + h * HD : HALF + (h + 1) * HD]
                v = packed[:, 2 * HALF + h * HD : 2 * HALF + (h + 1) * HD]
                d = dctx[:, h * HD : (h + 1) * HD]
                p = prob_ref[(band * 2 + pair) * MINE + h]
                dp = dot(d, v, ((1,), (1,)))
                dvs.append(dot(p.astype(BF16), d, ((0,), (0,))).astype(BF16))
                ds = p * (dp - jnp.sum(p * dp, axis=-1, keepdims=True))
                table_ref[h] += ds
                low = ds.astype(BF16)
                dqs.append((dot(low, k) * scale).astype(BF16))
                dks.append((dot(low, q, ((0,), (0,))) * scale).astype(BF16))
            dpk[pair * PAIR : (pair + 1) * PAIR, :] = jnp.concatenate(dqs + dks + dvs, axis=1)
        dsh = dot(dpk[...], w_ref[...], ((1,), (1,))).astype(BF16)
        back = dot(perm, dsh, ((0,), (0,))).astype(BF16)
        write_band(own_ref, give_ref, back, band, shift_h, shifts[2])
        return 0

    lax.fori_loop(0, BANDS, body, 0)


def joint_kernel(
    shifts, packed_ref, prob_ref, dctx_ref, w_ref, og_ref, give_ref,
    down_ref, dgot_ref, agot_ref, out_ref, score_ref,
    dpk, table, first, second, held, sent, slots, sums, seen,
    part_send, part_recv, local, ring_send, ring_recv, tok_send, tok_recv, cube_send, cube_recv,
):
    me = lax.axis_index("fsdp")
    core = me % 2
    chip = me // 2
    count = 16
    other = chip * 2 + (1 - core)
    barrier = pltpu.get_barrier_semaphore()
    for far in range(1, count):
        pl.semaphore_signal(
            barrier, inc=1, device_id={"fsdp": (me + far) % count}, device_id_type=MESH
        )
    pl.semaphore_wait(barrier, count - 1)

    def remote(src, dst, send, recv, target):
        return pltpu.make_async_remote_copy(
            src_ref=src, dst_ref=dst, send_sem=send, recv_sem=recv,
            device_id={"fsdp": target}, device_id_type=MESH,
        )

    a_copy = remote(give_ref, agot_ref, tok_send.at[0], tok_recv.at[0], other)
    a_copy.start()
    quarter = pl.ds(core * 4, 4)
    near = pltpu.make_async_copy(og_ref.at[:, core], held.at[quarter], local)
    far = remote(og_ref.at[:, 1 - core], held.at[quarter], part_send, part_recv, other)
    near.start()
    far.start()
    near.wait()
    far.wait()
    place = ring_place(chip)
    sides = (ring_chip(place + 1) * 2 + core, ring_chip(place - 1) * 2 + core)

    def hop(way, step):
        return remote(
            sent.at[way, step], slots.at[way, step], ring_send.at[way, step],
            ring_recv.at[way, step], sides[way],
        )

    def travel(step):
        for way in range(2):
            owner = ring_chip(place + (4 - step) * (1 - 2 * way))

            @pl.when(step > way)
            def _():
                hop(way, step - 1).wait_recv()
                sent[way, step] = (
                    held[owner].astype(F32) + slots[way, step - 1].astype(F32)
                ).astype(BF16)

            @pl.when(step == way)
            def _():
                sent[way, step] = held[owner]

            @pl.when(step >= way)
            def _():
                hop(way, step).start()

    backward_bands(shifts, packed_ref, prob_ref, dctx_ref, w_ref, first, table, dpk, travel)

    sums[0] = table[:, :64, :64] + table[:, 64:, 64:]

    def cube(step):
        peer = chip + (1 << step) * (1 - 2 * ((chip // (1 << step)) % 2))
        return remote(
            sums.at[step], seen.at[step], cube_send.at[step], cube_recv.at[step], peer * 2 + core
        )

    src, dst = first, second
    for step in range(3):
        cube(step).start()
        taken = (shifts[0] >> step) & 1
        back = 1 << step

        def roll(row, _):
            dst[row] = jnp.where(taken == 1, src[lax.rem(row + SIDE - back, SIDE)], src[row])
            return 0

        lax.fori_loop(0, SIDE, roll, 0)
        src, dst = dst, src
        if step == 2:
            half = SIDE // 2
            d_copy = remote(
                src.at[pl.ds((1 - core) * half, half)], dgot_ref, tok_send.at[1], tok_recv.at[1], other
            )
            d_copy.start()
        cube(step).wait()
        sums[step + 1] = sums[step] + seen[step]
    last = remote(sums.at[3], seen.at[3], cube_send.at[3], cube_recv.at[3], other)
    last.start()

    def keep(row, _):
        down_ref[row] = src[core * (SIDE // 2) + row]
        return 0

    lax.fori_loop(0, SIDE // 2, keep, 0)
    for way in range(2):
        hop(way, 3).wait_recv()
        for step in range(way, 4):
            hop(way, step).wait_send()
    out_ref[...] = held[chip].astype(F32) + slots[0, 3].astype(F32) + slots[1, 3].astype(F32)
    last.wait()
    score_ref[core] = sums[3]
    score_ref[1 - core] = seen[3]
    a_copy.wait()
    d_copy.wait()


def backward_bands(shifts, packed_ref, prob_ref, dctx_ref, w_ref, out_ref, table_ref, dpk, travel):
    shift_w = shifts[1]
    perm = band_permutation(shift_w)
    scale = HD**-0.5
    table_ref[...] = jnp.zeros_like(table_ref)

    def body(band, _):
        travel(band)
        for pair in range(2):
            rows = pl.ds(pl.multiple_of(band * BAND + pair * PAIR, PAIR), PAIR)
            packed = packed_ref[rows, :]
            dctx = dctx_ref[rows, :]
            dqs, dks, dvs = [], [], []
            for h in range(MINE):
                q = packed[:, h * HD : (h + 1) * HD]
                k = packed[:, HALF + h * HD : HALF + (h + 1) * HD]
                v = packed[:, 2 * HALF + h * HD : 2 * HALF + (h + 1) * HD]
                d = dctx[:, h * HD : (h + 1) * HD]
                p = prob_ref[(band * 2 + pair) * MINE + h]
                dp = dot(d, v, ((1,), (1,)))
                dvs.append(dot(p.astype(BF16), d, ((0,), (0,))).astype(BF16))
                ds = p * (dp - jnp.sum(p * dp, axis=-1, keepdims=True))
                table_ref[h] += ds
                low = ds.astype(BF16)
                dqs.append((dot(low, k) * scale).astype(BF16))
                dks.append((dot(low, q, ((0,), (0,))) * scale).astype(BF16))
            dpk[pair * PAIR : (pair + 1) * PAIR, :] = jnp.concatenate(dqs + dks + dvs, axis=1)
        dsh = dot(dpk[...], w_ref[...], ((1,), (1,))).astype(BF16)
        back = dot(perm, dsh, ((0,), (0,))).astype(BF16)
        for i in range(WIN):
            out_ref[band * WIN + i] = back[i * SIDE : (i + 1) * SIDE]
        return 0

    lax.fori_loop(0, BANDS, body, 0)


def norm_kernel(x_ref, o_ref):
    values = x_ref[...].astype(F32)
    centered = values - jnp.mean(values, axis=-1, keepdims=True)
    scale = lax.rsqrt(jnp.mean(centered * centered, axis=-1, keepdims=True) + 1e-05)
    o_ref[...] = (centered * scale).astype(BF16)


def norm_back_kernel(x_ref, a_ref, b_ref, o_ref):
    values = x_ref[...].astype(F32)
    centered = values - jnp.mean(values, axis=-1, keepdims=True)
    scale = lax.rsqrt(jnp.mean(centered * centered, axis=-1, keepdims=True) + 1e-05)
    xhat = centered * scale
    grad = a_ref[...].astype(F32) + b_ref[...].astype(F32)
    grad = grad.astype(BF16).astype(F32)
    mean_grad = jnp.mean(grad, axis=-1, keepdims=True)
    mean_cross = jnp.mean(grad * xhat, axis=-1, keepdims=True)
    o_ref[...] = (scale * (grad - mean_grad - xhat * mean_cross)).astype(BF16)


def rowwise(kernel, *arrays):
    rows, cols, width = arrays[0].shape
    step = 4
    spec = pl.BlockSpec((step, cols, width), lambda i: (i, 0, 0))
    return pl.pallas_call(
        kernel,
        out_shape=jax.ShapeDtypeStruct(arrays[0].shape, BF16),
        grid=(rows // step,),
        in_specs=[spec] * len(arrays),
        out_specs=spec,
        cost_estimate=pl.CostEstimate(
            flops=20 * rows * cols * width, bytes_accessed=2 * rows * cols * width * 3, transcendentals=0
        ),
    )(*arrays)


def whole(count):
    return [pl.BlockSpec(memory_space=pltpu.VMEM)] * count


def shape(dims, kind):
    return jax.ShapeDtypeStruct(dims, kind)


def offset_table(window):
    span = 2 * window - 1
    position = jnp.arange(window, dtype=jnp.int32)
    offset = position[:, None] - position[None, :] + window - 1
    return (offset[:, :, None] == jnp.arange(span, dtype=jnp.int32)[None, None, :]).astype(F32)


def both_halves(own, other, core):
    return jnp.where(
        core == 0, jnp.concatenate([own, other], axis=0), jnp.concatenate([other, own], axis=0)
    )


MESH = pl.DeviceIdType.MESH


def ring_place(chip):
    z = chip // 2
    return jnp.where(chip % 2 == 0, z, 7 - z)


def ring_chip(place):
    place = (place + 8) % 8
    return jnp.where(place < 4, 2 * place, 2 * (7 - place) + 1)


def gather_kernel(
    w_ref, ow_ref, x_ref, cot_ref, w_out, ow_out, x_out, cot_out, normed,
    tok_send, tok_recv, local, pair_send, pair_recv, ring_send, ring_recv, cross_send, cross_recv,
):
    me = lax.axis_index("fsdp")
    group = lax.axis_index("groups")
    core = me % 2
    chip = me // 2
    place = ring_place(chip)
    right = ring_chip(place + 1) * 2 + core
    left = ring_chip(place - 1) * 2 + core
    other = chip * 2 + (1 - core)

    barrier = pltpu.get_barrier_semaphore()
    for target in ({"fsdp": other}, {"fsdp": right}, {"fsdp": left}, {"groups": 1 - group}):
        pl.semaphore_signal(barrier, inc=1, device_id=target, device_id_type=MESH)
    pl.semaphore_wait(barrier, 4)

    def remote(src, dst, send, recv, target):
        return pltpu.make_async_remote_copy(
            src_ref=src, dst_ref=dst, send_sem=send, recv_sem=recv, device_id=target, device_id_type=MESH
        )

    rows = w_ref.shape[0]
    own_rows = pl.ds(pl.multiple_of((chip * 2 + core) * rows, rows), rows)
    pairs, locals_ = [], []
    for kind in range(3):
        dst = w_out.at[own_rows, pl.ds(kind * HALF, HALF)]

        def columns(which):
            return w_ref.at[:, pl.ds(pl.multiple_of(kind * 2 * HALF + which * HALF, HALF), HALF)]

        pairs.append(
            remote(columns(1 - core), dst, pair_send.at[kind], pair_recv.at[kind], {"fsdp": other})
        )
        locals_.append(pltpu.make_async_copy(columns(core), dst, local.at[kind]))
    locals_.append(pltpu.make_async_copy(ow_ref, ow_out.at[chip, core], local.at[3]))
    for copy in pairs + locals_:
        copy.start()
    cot_far = remote(cot_ref, cot_out.at[core], tok_send.at[0], tok_recv.at[0], {"fsdp": other})
    cot_near = pltpu.make_async_copy(cot_ref, cot_out.at[core], local.at[4])
    for copy in locals_:
        copy.wait()
    for copy in pairs:
        copy.wait()

    third = 2 * rows // 3
    thin = ow_ref.shape[0] // 3

    def piece(name, chunk):
        part = group if name[1] == "m" else 2
        if name[0] == "w":
            start = pl.multiple_of(chunk * (2 * rows) + part * third, third)
            return w_out.at[pl.ds(start, third), :]
        return ow_out.at[chunk, core, pl.ds(pl.multiple_of(part * thin, thin), thin), :]

    names = ("wm", "wc", "om", "oc")

    def carried(way, step):
        if step < 4:
            return names
        return ("wm", "om") if way == 0 else ("wc", "oc")

    def hop(way, step, name):
        chunk = ring_chip(place - (step - 1) if way == 0 else place + (step - 1))
        ref = piece(name, chunk)
        i = names.index(name)
        return remote(
            ref, ref, ring_send.at[way, step - 1, i], ring_recv.at[way, step - 1, i],
            {"fsdp": right if way == 0 else left},
        )

    def arrival(way, step, name):
        chunk = ring_chip(place - step if way == 0 else place + step)
        ref = piece(name, chunk)
        i = names.index(name)
        return remote(
            ref, ref, ring_send.at[way, step - 1, i], ring_recv.at[way, step - 1, i],
            {"fsdp": right if way == 0 else left},
        )

    def cross(way, step, name, mine):
        chunk = ring_chip(place - step if way == 0 else place + step)
        part = group if mine else 1 - group
        if name == "wm":
            start = pl.multiple_of(chunk * (2 * rows) + part * third, third)
            ref = w_out.at[pl.ds(start, third), :]
        else:
            ref = ow_out.at[chunk, core, pl.ds(pl.multiple_of(part * thin, thin), thin), :]
        i = 0 if name == "wm" else 1
        return remote(
            ref, ref, cross_send.at[way, step - 1, i], cross_recv.at[way, step - 1, i],
            {"groups": 1 - group},
        )

    for name in names:
        for way in range(2):
            hop(way, 1, name).start()
    cot_far.start()
    cot_near.start()

    def norm_row(i, _):
        values = x_ref[i].astype(F32)
        centered = values - jnp.mean(values, axis=-1, keepdims=True)
        scale = lax.rsqrt(jnp.mean(centered * centered, axis=-1, keepdims=True) + 1e-05)
        normed[i] = (centered * scale).astype(BF16)
        return 0

    lax.fori_loop(0, x_ref.shape[0], norm_row, 0)
    x_far = remote(normed, x_out.at[core], tok_send.at[1], tok_recv.at[1], {"fsdp": other})
    x_near = pltpu.make_async_copy(normed, x_out.at[core], local.at[5])
    x_far.start()
    x_near.start()

    crossed = []
    for step in range(1, 5):
        for name in names:
            for way in range(2):
                if name not in carried(way, step):
                    continue
                arrival(way, step, name).wait_recv()
                if step < 4 and name in carried(way, step + 1):
                    hop(way, step + 1, name).start()
                if name[1] == "m":
                    cross(way, step, name, True).start()
                    crossed.append((way, step, name))
    for way, step, name in crossed:
        cross(way, step, name, False).wait_recv()
    half = ow_out.shape[0] // 2
    give = ow_out.at[pl.ds((1 - core) * half, half), core]
    swap = remote(give, give, pair_send.at[3], pair_recv.at[3], {"fsdp": other})
    swap.start()
    for step in range(1, 5):
        for way in range(2):
            for name in carried(way, step):
                hop(way, step, name).wait_send()
    for way, step, name in crossed:
        cross(way, step, name, True).wait_send()
    cot_far.wait()
    cot_near.wait()
    x_far.wait()
    x_near.wait()
    swap.wait()


def gathered(fields, in_weight, out_weight, cotangent):
    row_count, col_count, width = fields.shape
    count = lax.axis_size("fsdp")
    anywhere = pl.BlockSpec(memory_space=pl.ANY)
    dma = pltpu.SemaphoreType.DMA
    return pl.pallas_call(
        gather_kernel,
        out_shape=(
            shape((width, 3 * HALF), BF16),
            shape((count // 2, 2, out_weight.shape[0], width), BF16),
            shape((2, row_count, col_count, width), BF16),
            shape((2, row_count, col_count, width), BF16),
        ),
        in_specs=[anywhere, anywhere, pl.BlockSpec(memory_space=pltpu.VMEM), anywhere],
        out_specs=(anywhere,) * 4,
        scratch_shapes=[
            pltpu.VMEM(fields.shape, BF16),
            dma((2,)), dma((2,)), dma((6,)), dma((4,)), dma((4,)),
            dma((2, 4, 4)), dma((2, 4, 4)), dma((2, 4, 2)), dma((2, 4, 2)),
        ],
        compiler_params=pltpu.CompilerParams(
            collective_id=0, has_side_effects=True, vmem_limit_bytes=56 * 1024 * 1024
        ),
        cost_estimate=pl.CostEstimate(flops=10**8, bytes_accessed=10**8, transcendentals=0),
    )(in_weight, out_weight, fields, cotangent)


def joint_call(scalars, packed, prob, dctx, w_full, og, give):
    dma = pltpu.SemaphoreType.DMA
    area = WIN * WIN
    return pl.pallas_call(
        joint_kernel,
        out_shape=(
            shape(give.shape, BF16),
            shape(give.shape, BF16),
            shape(give.shape, BF16),
            shape(og.shape[1:], F32),
            shape((2, MINE, area, area), F32),
        ),
        in_specs=[pl.BlockSpec(memory_space=pltpu.SMEM)] + whole(6),
        out_specs=tuple(whole(5)),
        scratch_shapes=[
            pltpu.VMEM((BAND, 3 * HALF), BF16),
            pltpu.VMEM((MINE, PAIR, PAIR), F32),
            pltpu.VMEM((SIDE, SIDE, give.shape[2]), BF16),
            pltpu.VMEM((SIDE, SIDE, give.shape[2]), BF16),
            pltpu.VMEM((8,) + og.shape[1:], BF16),
            pltpu.VMEM((2, 4) + og.shape[1:], BF16),
            pltpu.VMEM((2, 4) + og.shape[1:], BF16),
            pltpu.VMEM((4, MINE, area, area), F32),
            pltpu.VMEM((4, MINE, area, area), F32),
            dma, dma, dma, dma((2, 4)), dma((2, 4)), dma((2,)), dma((2,)), dma((4,)), dma((4,)),
        ],
        compiler_params=pltpu.CompilerParams(
            collective_id=1, has_side_effects=True, vmem_limit_bytes=VMEM_LIMIT
        ),
        cost_estimate=pl.CostEstimate(flops=10**10, bytes_accessed=2 * 10**7, transcendentals=0),
    )(scalars, packed, prob, dctx, w_full, og.reshape((4, 2) + og.shape[1:]), give)


def gathered_plain(fields, in_weight, out_weight, cotangent):
    core = lax.axis_index("fsdp") % 2
    groups = same_core_groups()
    split = in_weight.reshape(in_weight.shape[0], 3, 2, HALF)
    keep = lax.dynamic_index_in_dim(split, core, 2, False).reshape(-1, 3 * HALF)
    give = lax.dynamic_index_in_dim(split, 1 - core, 2, False).reshape(-1, 3 * HALF)
    w_chip = both_halves(keep, partner(give), core)
    w_full = lax.all_gather(w_chip, "fsdp", axis=0, tiled=True, axis_index_groups=groups)
    ow_all = lax.all_gather(out_weight, "fsdp", axis=0, tiled=True)
    normed = rowwise(norm_kernel, fields)
    x_all = both_halves(normed, partner(normed), core)
    cot_all = both_halves(cotangent, partner(cotangent), core)
    return w_full, ow_all, x_all, cot_all


def shards(fields, shifts, in_weight, out_weight, bias_table, cotangent):
    row_count, col_count, width = fields.shape
    core = lax.axis_index("fsdp") % 2
    chips = lax.axis_size("fsdp") // 2
    span = 2 * WIN - 1
    area = WIN * WIN

    gather = gathered if 2 * chips == 16 else gathered_plain
    w_full, ow_all, x_all, cot_all = gather(fields, in_weight, out_weight, cotangent)
    ow_full = ow_all.reshape(2 * HALF, width)
    x_all = x_all.reshape(SIDE, col_count, width)
    cot_all = cot_all.reshape(SIDE, col_count, width)
    joint = 2 * chips == 16
    turn = 0 * core if joint else lax.axis_index("fsdp") // 2
    scalars = jnp.concatenate([shifts, jnp.stack([core, turn])]).astype(jnp.int32)

    table = offset_table(WIN)
    own_table = lax.dynamic_slice_in_dim(bias_table, core * MINE, MINE, 0)
    bias = jnp.einsum(
        "huv,pqu,rsv->hprqs",
        own_table.reshape(MINE, span, span),
        table,
        table,
        precision=lax.Precision.HIGHEST,
    ).reshape(MINE, area, area)
    bias = jnp.tile(bias, (1, 2, 2))

    tokens = SIDE * SIDE
    blocks = BANDS * 2 * MINE
    params = pltpu.CompilerParams(vmem_limit_bytes=VMEM_LIMIT)
    smem = pl.BlockSpec(memory_space=pltpu.SMEM)
    packed, prob, dctx, a_own, a_give, og = pl.pallas_call(
        forward_kernel,
        out_shape=(
            shape((tokens, 3 * HALF), BF16),
            shape((blocks, PAIR, PAIR), F32),
            shape((tokens, HALF), BF16),
            shape(fields.shape, BF16),
            shape(fields.shape, BF16),
            shape((chips, HALF // chips, width), BF16),
        ),
        in_specs=[smem] + whole(5),
        out_specs=tuple(whole(6)),
        scratch_shapes=[pltpu.VMEM((chips, HALF // chips, width), F32)],
        compiler_params=params,
        cost_estimate=pl.CostEstimate(flops=10**10, bytes_accessed=2 * 10**7, transcendentals=10**6),
    )(scalars, x_all, cot_all, w_full, ow_full, bias)

    terms = []
    for far in range(0 if joint else chips):
        route = [
            (2 * c + k, k * chips + (c + far) % chips) for c in range(chips) for k in range(2)
        ]
        terms.append(lax.ppermute(og[far], "fsdp", route))
    if joint:
        d_own, d_got, a_got, out_grad, score = joint_call(
            scalars, packed, prob, dctx, w_full, og, a_give
        )
        attended = (a_own.astype(F32) + a_got.astype(F32)).astype(BF16)
        fields_gradient = rowwise(norm_back_kernel, fields, d_own, d_got)
        local = score.reshape(HEADS, WIN, WIN, WIN, WIN)
        table_grad = jnp.einsum(
            "hprqs,pqu,rsv->huv", local, table, table, precision=lax.Precision.HIGHEST
        ).reshape(HEADS, span * span)
        return (attended, fields_gradient, out_grad, table_grad)
    a_got = partner(a_give)

    d_own, d_give, score = pl.pallas_call(
        backward_kernel,
        out_shape=(
            shape(fields.shape, BF16),
            shape(fields.shape, BF16),
            shape((MINE, PAIR, PAIR), F32),
        ),
        in_specs=[smem] + whole(4),
        out_specs=tuple(whole(3)),
        scratch_shapes=[pltpu.VMEM((BAND, 3 * HALF), BF16)],
        compiler_params=params,
        cost_estimate=pl.CostEstimate(flops=10**10, bytes_accessed=2 * 10**7, transcendentals=10**6),
    )(scalars, packed, prob, dctx, w_full)

    d_got = partner(d_give)
    attended = (a_own.astype(F32) + a_got.astype(F32)).astype(BF16)
    fields_gradient = rowwise(norm_back_kernel, fields, d_own, d_got)
    out_grad = functools.reduce(jnp.add, [term.astype(F32) for term in terms])

    local = (score[:, :area, :area] + score[:, area:, area:]).reshape(MINE, WIN, WIN, WIN, WIN)
    own_grad = jnp.einsum(
        "hprqs,pqu,rsv->huv", local, table, table, precision=lax.Precision.HIGHEST
    ).reshape(MINE, span * span)
    padded = lax.dynamic_update_slice_in_dim(
        jnp.zeros((HEADS, span * span), F32), own_grad, core * MINE, 0
    )
    table_grad = padded
    count, stride = 2 * chips, 1
    while stride < count:
        route = [(d, d ^ stride) for d in range(count)]
        table_grad = table_grad + lax.ppermute(table_grad, "fsdp", route)
        stride *= 2
    return (attended, fields_gradient, out_grad, table_grad)


def solution(mesh):
    in_specs = (
        P(("groups", "fsdp"), None, None),
        P(),
        P("fsdp", None),
        P("fsdp", None),
        P(),
        P(("groups", "fsdp"), None, None),
    )
    out_specs = (
        P(("groups", "fsdp"), None, None),
        P(("groups", "fsdp"), None, None),
        P(("groups", "fsdp"), None),
        P("groups", None),
    )
    return jax.shard_map(shards, mesh=mesh, in_specs=in_specs, out_specs=out_specs, check_vma=False)
```

```python
import functools

import jax
import jax.numpy as jnp
from jax import lax
from jax.experimental import pallas as pl
from jax.experimental.pallas import tpu as pltpu
from jax.sharding import PartitionSpec as P

HEADS = 12
HD = 64
WIN = 8
SIDE = 32
MINE = HEADS // 2
HALF = MINE * HD
BAND = WIN * SIDE
PAIR = 2 * WIN * WIN
BANDS = SIDE // WIN
VMEM_LIMIT = 60 * 1024 * 1024
F32 = jnp.float32
BF16 = jnp.bfloat16


def dot(a, b, dims=((1,), (0,))):
    return lax.dot_general(a, b, (dims, ((), ())), preferred_element_type=F32)


def partner(block):
    count = lax.axis_size("fsdp")
    return lax.ppermute(block, "fsdp", [(d, d ^ 1) for d in range(count)])


def same_core_groups():
    count = lax.axis_size("fsdp")
    return [list(range(0, count, 2)), list(range(1, count, 2))]


def band_permutation(shift_w):
    t = lax.broadcasted_iota(jnp.int32, (BAND, BAND), 0)
    s = lax.broadcasted_iota(jnp.int32, (BAND, BAND), 1)
    row = (t >> 3) & 7
    col = ((t >> 6) * WIN + (t & 7) + shift_w) & (SIDE - 1)
    return (row * SIDE + col == s).astype(F32).astype(BF16)


def pair_labels(band, pair, shift_h, shift_w, axis):
    shape = (PAIR, 1) if axis == 0 else (1, PAIR)
    t = lax.broadcasted_iota(jnp.int32, shape, axis)
    which = t >> 6
    row = band * WIN + ((t >> 3) & 7)
    col = pair * 2 * WIN + which * WIN + (t & 7)

    def label(index, shift):
        return jnp.where(index >= SIDE - WIN, 1, 0) + jnp.where(index >= SIDE - shift, 1, 0)

    return which * 16 + 3 * label(row, shift_h) + label(col, shift_w)


def read_band(ref, band, shift_h):
    rows = [ref[(band * WIN + i + shift_h) & (SIDE - 1)] for i in range(WIN)]
    return jnp.concatenate(rows, axis=0)


def write_band(own_ref, give_ref, value, band, shift_h, core):
    half = SIDE // 2
    for i in range(WIN):
        row = (band * WIN + i + shift_h) & (SIDE - 1)
        inside = row & (half - 1)
        mine = row // half == core

        @pl.when(mine)
        def _():
            own_ref[inside] = value[i * SIDE : (i + 1) * SIDE]

        @pl.when(jnp.logical_not(mine))
        def _():
            give_ref[inside] = value[i * SIDE : (i + 1) * SIDE]


def forward_kernel(
    shifts, x_ref, cot_ref, w_ref, ow_ref, bias_ref, packed_ref, prob_ref, dctx_ref, own_ref, give_ref, og_out, og_ref
):
    shift_h = shifts[0]
    shift_w = shifts[1]
    core = shifts[2]
    perm = band_permutation(shift_w)
    ow = ow_ref.at[pl.ds(pl.multiple_of(core * HALF, HALF), HALF), :]

    def body(band, _):
        tokens = pl.ds(pl.multiple_of(band * BAND, BAND), BAND)
        xs = dot(perm, read_band(x_ref, band, shift_h)).astype(BF16)
        packed = dot(xs, w_ref[...]).astype(BF16)
        packed_ref[tokens, :] = packed
        cot = dot(perm, read_band(cot_ref, band, shift_h)).astype(BF16)
        dctx_ref[tokens, :] = dot(cot, ow[...], ((1,), (1,))).astype(BF16)
        pairs = []
        for pair in range(2):
            rows = slice(pair * PAIR, (pair + 1) * PAIR)
            allowed = pair_labels(band, pair, shift_h, shift_w, 0) == pair_labels(
                band, pair, shift_h, shift_w, 1
            )
            heads = []
            for h in range(MINE):
                q = packed[rows, h * HD : (h + 1) * HD]
                k = packed[rows, HALF + h * HD : HALF + (h + 1) * HD]
                v = packed[rows, 2 * HALF + h * HD : 2 * HALF + (h + 1) * HD]
                s = dot(q, k, ((1,), (1,))) * (HD**-0.5) + bias_ref[h]
                s = jnp.where(allowed, s, -1e9)
                e = jnp.exp(s - jnp.max(s, axis=-1, keepdims=True))
                p = e / jnp.sum(e, axis=-1, keepdims=True)
                prob_ref[(band * 2 + pair) * MINE + h] = p
                heads.append(dot(p.astype(BF16), v).astype(BF16))
            pairs.append(jnp.concatenate(heads, axis=1))
        ctx = jnp.concatenate(pairs, axis=0)
        grad = dot(ctx, cot, ((0,), (0,)))

        @pl.when(band == 0)
        def _():
            og_ref[...] = grad.reshape(og_ref.shape)

        @pl.when(band > 0)
        def _():
            og_ref[...] += grad.reshape(og_ref.shape)

        proj = dot(ctx, ow[...]).astype(BF16)
        back = dot(perm, proj, ((0,), (0,))).astype(BF16)
        write_band(own_ref, give_ref, back, band, shift_h, core)
        return 0

    lax.fori_loop(0, BANDS, body, 0)
    parts, rows, _ = og_out.shape

    def order(i, _):
        owner = lax.rem(shifts[3] + i, parts)
        og_out[i] = og_ref[owner].astype(BF16)
        return 0

    lax.fori_loop(0, parts, order, 0)


def backward_kernel(shifts, packed_ref, prob_ref, dctx_ref, w_ref, own_ref, give_ref, table_ref, dpk):
    shift_h = shifts[0]
    shift_w = shifts[1]
    perm = band_permutation(shift_w)
    scale = HD**-0.5
    table_ref[...] = jnp.zeros_like(table_ref)

    def body(band, _):
        for pair in range(2):
            rows = pl.ds(pl.multiple_of(band * BAND + pair * PAIR, PAIR), PAIR)
            packed = packed_ref[rows, :]
            dctx = dctx_ref[rows, :]
            dqs, dks, dvs = [], [], []
            for h in range(MINE):
                q = packed[:, h * HD : (h + 1) * HD]
                k = packed[:, HALF + h * HD : HALF + (h + 1) * HD]
                v = packed[:, 2 * HALF + h * HD : 2 * HALF + (h + 1) * HD]
                d = dctx[:, h * HD : (h + 1) * HD]
                p = prob_ref[(band * 2 + pair) * MINE + h]
                dp = dot(d, v, ((1,), (1,)))
                dvs.append(dot(p.astype(BF16), d, ((0,), (0,))).astype(BF16))
                ds = p * (dp - jnp.sum(p * dp, axis=-1, keepdims=True))
                table_ref[h] += ds
                low = ds.astype(BF16)
                dqs.append((dot(low, k) * scale).astype(BF16))
                dks.append((dot(low, q, ((0,), (0,))) * scale).astype(BF16))
            dpk[pair * PAIR : (pair + 1) * PAIR, :] = jnp.concatenate(dqs + dks + dvs, axis=1)
        dsh = dot(dpk[...], w_ref[...], ((1,), (1,))).astype(BF16)
        back = dot(perm, dsh, ((0,), (0,))).astype(BF16)
        write_band(own_ref, give_ref, back, band, shift_h, shifts[2])
        return 0

    lax.fori_loop(0, BANDS, body, 0)


def joint_kernel(
    shifts, packed_ref, prob_ref, dctx_ref, w_ref, og_ref, give_ref,
    down_ref, dgot_ref, agot_ref, out_ref, score_ref,
    dpk, table, first, second, held, sent, slots, sums, seen,
    part_send, part_recv, local, ring_send, ring_recv, tok_send, tok_recv, cube_send, cube_recv,
):
    me = lax.axis_index("fsdp")
    core = me % 2
    chip = me // 2
    count = 16
    other = chip * 2 + (1 - core)
    barrier = pltpu.get_barrier_semaphore()
    for far in range(1, count):
        pl.semaphore_signal(
            barrier, inc=1, device_id={"fsdp": (me + far) % count}, device_id_type=MESH
        )
    pl.semaphore_wait(barrier, count - 1)

    def remote(src, dst, send, recv, target):
        return pltpu.make_async_remote_copy(
            src_ref=src, dst_ref=dst, send_sem=send, recv_sem=recv,
            device_id={"fsdp": target}, device_id_type=MESH,
        )

    a_copy = remote(give_ref, agot_ref, tok_send.at[0], tok_recv.at[0], other)
    quarter = pl.ds(core * 4, 4)
    near = pltpu.make_async_copy(og_ref.at[:, core], held.at[quarter], local)
    far = remote(og_ref.at[:, 1 - core], held.at[quarter], part_send, part_recv, other)
    near.start()
    far.start()
    near.wait()
    far.wait()
    a_copy.start()
    place = ring_place(chip)
    sides = (ring_chip(place + 1) * 2 + core, ring_chip(place - 1) * 2 + core)

    def hop(way, step):
        return remote(
            sent.at[way, step], slots.at[way, step], ring_send.at[way, step],
            ring_recv.at[way, step], sides[way],
        )

    def travel(step):
        for way in range(2):
            owner = ring_chip(place + (4 - step) * (1 - 2 * way))

            @pl.when(step > way)
            def _():
                hop(way, step - 1).wait_recv()
                sent[way, step] = (
                    held[owner].astype(F32) + slots[way, step - 1].astype(F32)
                ).astype(BF16)

            @pl.when(step == way)
            def _():
                sent[way, step] = held[owner]

            @pl.when(step >= way)
            def _():
                hop(way, step).start()

    backward_bands(shifts, packed_ref, prob_ref, dctx_ref, w_ref, first, table, dpk, travel)

    sums[0] = table[:, :64, :64] + table[:, 64:, 64:]

    def cube(step):
        peer = chip + (1 << step) * (1 - 2 * ((chip // (1 << step)) % 2))
        return remote(
            sums.at[step], seen.at[step], cube_send.at[step], cube_recv.at[step], peer * 2 + core
        )

    src, dst = first, second
    for step in range(3):
        cube(step).start()
        taken = (shifts[0] >> step) & 1
        back = 1 << step

        def roll(row, _):
            dst[row] = jnp.where(taken == 1, src[lax.rem(row + SIDE - back, SIDE)], src[row])
            return 0

        lax.fori_loop(0, SIDE, roll, 0)
        src, dst = dst, src
        if step == 2:
            half = SIDE // 2
            d_copy = remote(
                src.at[pl.ds((1 - core) * half, half)], dgot_ref, tok_send.at[1], tok_recv.at[1], other
            )
            d_copy.start()
        cube(step).wait()
        sums[step + 1] = sums[step] + seen[step]
    last = remote(sums.at[3], seen.at[3], cube_send.at[3], cube_recv.at[3], other)
    last.start()

    def keep(row, _):
        down_ref[row] = src[core * (SIDE // 2) + row]
        return 0

    lax.fori_loop(0, SIDE // 2, keep, 0)
    for way in range(2):
        hop(way, 3).wait_recv()
        for step in range(way, 4):
            hop(way, step).wait_send()
    out_ref[...] = held[chip].astype(F32) + slots[0, 3].astype(F32) + slots[1, 3].astype(F32)
    last.wait()
    score_ref[core] = sums[3]
    score_ref[1 - core] = seen[3]
    a_copy.wait()
    d_copy.wait()


def backward_bands(shifts, packed_ref, prob_ref, dctx_ref, w_ref, out_ref, table_ref, dpk, travel):
    shift_w = shifts[1]
    perm = band_permutation(shift_w)
    scale = HD**-0.5
    table_ref[...] = jnp.zeros_like(table_ref)

    def body(band, _):
        travel(band)
        for pair in range(2):
            rows = pl.ds(pl.multiple_of(band * BAND + pair * PAIR, PAIR), PAIR)
            packed = packed_ref[rows, :]
            dctx = dctx_ref[rows, :]
            dqs, dks, dvs = [], [], []
            for h in range(MINE):
                q = packed[:, h * HD : (h + 1) * HD]
                k = packed[:, HALF + h * HD : HALF + (h + 1) * HD]
                v = packed[:, 2 * HALF + h * HD : 2 * HALF + (h + 1) * HD]
                d = dctx[:, h * HD : (h + 1) * HD]
                p = prob_ref[(band * 2 + pair) * MINE + h]
                dp = dot(d, v, ((1,), (1,)))
                dvs.append(dot(p.astype(BF16), d, ((0,), (0,))).astype(BF16))
                ds = p * (dp - jnp.sum(p * dp, axis=-1, keepdims=True))
                table_ref[h] += ds
                low = ds.astype(BF16)
                dqs.append((dot(low, k) * scale).astype(BF16))
                dks.append((dot(low, q, ((0,), (0,))) * scale).astype(BF16))
            dpk[pair * PAIR : (pair + 1) * PAIR, :] = jnp.concatenate(dqs + dks + dvs, axis=1)
        dsh = dot(dpk[...], w_ref[...], ((1,), (1,))).astype(BF16)
        back = dot(perm, dsh, ((0,), (0,))).astype(BF16)
        for i in range(WIN):
            out_ref[band * WIN + i] = back[i * SIDE : (i + 1) * SIDE]
        return 0

    lax.fori_loop(0, BANDS, body, 0)


def norm_kernel(x_ref, o_ref):
    values = x_ref[...].astype(F32)
    centered = values - jnp.mean(values, axis=-1, keepdims=True)
    scale = lax.rsqrt(jnp.mean(centered * centered, axis=-1, keepdims=True) + 1e-05)
    o_ref[...] = (centered * scale).astype(BF16)


def norm_back_kernel(x_ref, a_ref, b_ref, o_ref):
    values = x_ref[...].astype(F32)
    centered = values - jnp.mean(values, axis=-1, keepdims=True)
    scale = lax.rsqrt(jnp.mean(centered * centered, axis=-1, keepdims=True) + 1e-05)
    xhat = centered * scale
    grad = a_ref[...].astype(F32) + b_ref[...].astype(F32)
    grad = grad.astype(BF16).astype(F32)
    mean_grad = jnp.mean(grad, axis=-1, keepdims=True)
    mean_cross = jnp.mean(grad * xhat, axis=-1, keepdims=True)
    o_ref[...] = (scale * (grad - mean_grad - xhat * mean_cross)).astype(BF16)


def rowwise(kernel, *arrays):
    rows, cols, width = arrays[0].shape
    step = 4
    spec = pl.BlockSpec((step, cols, width), lambda i: (i, 0, 0))
    return pl.pallas_call(
        kernel,
        out_shape=jax.ShapeDtypeStruct(arrays[0].shape, BF16),
        grid=(rows // step,),
        in_specs=[spec] * len(arrays),
        out_specs=spec,
        cost_estimate=pl.CostEstimate(
            flops=20 * rows * cols * width, bytes_accessed=2 * rows * cols * width * 3, transcendentals=0
        ),
    )(*arrays)


def whole(count):
    return [pl.BlockSpec(memory_space=pltpu.VMEM)] * count


def shape(dims, kind):
    return jax.ShapeDtypeStruct(dims, kind)


def offset_table(window):
    span = 2 * window - 1
    position = jnp.arange(window, dtype=jnp.int32)
    offset = position[:, None] - position[None, :] + window - 1
    return (offset[:, :, None] == jnp.arange(span, dtype=jnp.int32)[None, None, :]).astype(F32)


def both_halves(own, other, core):
    return jnp.where(
        core == 0, jnp.concatenate([own, other], axis=0), jnp.concatenate([other, own], axis=0)
    )


MESH = pl.DeviceIdType.MESH


def ring_place(chip):
    z = chip // 2
    return jnp.where(chip % 2 == 0, z, 7 - z)


def ring_chip(place):
    place = (place + 8) % 8
    return jnp.where(place < 4, 2 * place, 2 * (7 - place) + 1)


def gather_kernel(
    w_ref, ow_ref, x_ref, cot_ref, w_out, ow_out, x_out, cot_out, normed,
    tok_send, tok_recv, local, pair_send, pair_recv, ring_send, ring_recv, cross_send, cross_recv,
):
    me = lax.axis_index("fsdp")
    group = lax.axis_index("groups")
    core = me % 2
    chip = me // 2
    place = ring_place(chip)
    right = ring_chip(place + 1) * 2 + core
    left = ring_chip(place - 1) * 2 + core
    other = chip * 2 + (1 - core)

    barrier = pltpu.get_barrier_semaphore()
    for target in ({"fsdp": other}, {"fsdp": right}, {"fsdp": left}, {"groups": 1 - group}):
        pl.semaphore_signal(barrier, inc=1, device_id=target, device_id_type=MESH)
    pl.semaphore_wait(barrier, 4)

    def remote(src, dst, send, recv, target):
        return pltpu.make_async_remote_copy(
            src_ref=src, dst_ref=dst, send_sem=send, recv_sem=recv, device_id=target, device_id_type=MESH
        )

    rows = w_ref.shape[0]
    own_rows = pl.ds(pl.multiple_of((chip * 2 + core) * rows, rows), rows)
    pairs, locals_ = [], []
    for kind in range(3):
        dst = w_out.at[own_rows, pl.ds(kind * HALF, HALF)]

        def columns(which):
            return w_ref.at[:, pl.ds(pl.multiple_of(kind * 2 * HALF + which * HALF, HALF), HALF)]

        pairs.append(
            remote(columns(1 - core), dst, pair_send.at[kind], pair_recv.at[kind], {"fsdp": other})
        )
        locals_.append(pltpu.make_async_copy(columns(core), dst, local.at[kind]))
    locals_.append(pltpu.make_async_copy(ow_ref, ow_out.at[chip, core], local.at[3]))
    for copy in pairs + locals_:
        copy.start()
    cot_far = remote(cot_ref, cot_out.at[core], tok_send.at[0], tok_recv.at[0], {"fsdp": other})
    cot_near = pltpu.make_async_copy(cot_ref, cot_out.at[core], local.at[4])
    for copy in locals_:
        copy.wait()
    for copy in pairs:
        copy.wait()

    third = 2 * rows // 3
    thin = ow_ref.shape[0] // 3

    def piece(name, chunk):
        part = group if name[1] == "m" else 2
        if name[0] == "w":
            start = pl.multiple_of(chunk * (2 * rows) + part * third, third)
            return w_out.at[pl.ds(start, third), :]
        return ow_out.at[chunk, core, pl.ds(pl.multiple_of(part * thin, thin), thin), :]

    names = ("wm", "wc", "om", "oc")

    def carried(way, step):
        if step < 4:
            return names
        return ("wm", "om") if way == 0 else ("wc", "oc")

    def hop(way, step, name):
        chunk = ring_chip(place - (step - 1) if way == 0 else place + (step - 1))
        ref = piece(name, chunk)
        i = names.index(name)
        return remote(
            ref, ref, ring_send.at[way, step - 1, i], ring_recv.at[way, step - 1, i],
            {"fsdp": right if way == 0 else left},
        )

    def arrival(way, step, name):
        chunk = ring_chip(place - step if way == 0 else place + step)
        ref = piece(name, chunk)
        i = names.index(name)
        return remote(
            ref, ref, ring_send.at[way, step - 1, i], ring_recv.at[way, step - 1, i],
            {"fsdp": right if way == 0 else left},
        )

    def cross(way, step, name, mine):
        chunk = ring_chip(place - step if way == 0 else place + step)
        part = group if mine else 1 - group
        if name == "wm":
            start = pl.multiple_of(chunk * (2 * rows) + part * third, third)
            ref = w_out.at[pl.ds(start, third), :]
        else:
            ref = ow_out.at[chunk, core, pl.ds(pl.multiple_of(part * thin, thin), thin), :]
        i = 0 if name == "wm" else 1
        return remote(
            ref, ref, cross_send.at[way, step - 1, i], cross_recv.at[way, step - 1, i],
            {"groups": 1 - group},
        )

    for name in names:
        for way in range(2):
            hop(way, 1, name).start()
    cot_far.start()
    cot_near.start()

    def norm_row(i, _):
        values = x_ref[i].astype(F32)
        centered = values - jnp.mean(values, axis=-1, keepdims=True)
        scale = lax.rsqrt(jnp.mean(centered * centered, axis=-1, keepdims=True) + 1e-05)
        normed[i] = (centered * scale).astype(BF16)
        return 0

    lax.fori_loop(0, x_ref.shape[0], norm_row, 0)
    x_far = remote(normed, x_out.at[core], tok_send.at[1], tok_recv.at[1], {"fsdp": other})
    x_near = pltpu.make_async_copy(normed, x_out.at[core], local.at[5])
    x_far.start()
    x_near.start()

    crossed = []
    for step in range(1, 5):
        for name in names:
            for way in range(2):
                if name not in carried(way, step):
                    continue
                arrival(way, step, name).wait_recv()
                if step < 4 and name in carried(way, step + 1):
                    hop(way, step + 1, name).start()
                if name[1] == "m":
                    cross(way, step, name, True).start()
                    crossed.append((way, step, name))
    for way, step, name in crossed:
        cross(way, step, name, False).wait_recv()
    half = ow_out.shape[0] // 2
    give = ow_out.at[pl.ds((1 - core) * half, half), core]
    swap = remote(give, give, pair_send.at[3], pair_recv.at[3], {"fsdp": other})
    swap.start()
    for step in range(1, 5):
        for way in range(2):
            for name in carried(way, step):
                hop(way, step, name).wait_send()
    for way, step, name in crossed:
        cross(way, step, name, True).wait_send()
    cot_far.wait()
    cot_near.wait()
    x_far.wait()
    x_near.wait()
    swap.wait()


def gathered(fields, in_weight, out_weight, cotangent):
    row_count, col_count, width = fields.shape
    count = lax.axis_size("fsdp")
    anywhere = pl.BlockSpec(memory_space=pl.ANY)
    dma = pltpu.SemaphoreType.DMA
    return pl.pallas_call(
        gather_kernel,
        out_shape=(
            shape((width, 3 * HALF), BF16),
            shape((count // 2, 2, out_weight.shape[0], width), BF16),
            shape((2, row_count, col_count, width), BF16),
            shape((2, row_count, col_count, width), BF16),
        ),
        in_specs=[anywhere, anywhere, pl.BlockSpec(memory_space=pltpu.VMEM), anywhere],
        out_specs=(anywhere,) * 4,
        scratch_shapes=[
            pltpu.VMEM(fields.shape, BF16),
            dma((2,)), dma((2,)), dma((6,)), dma((4,)), dma((4,)),
            dma((2, 4, 4)), dma((2, 4, 4)), dma((2, 4, 2)), dma((2, 4, 2)),
        ],
        compiler_params=pltpu.CompilerParams(
            collective_id=0, has_side_effects=True, vmem_limit_bytes=56 * 1024 * 1024
        ),
        cost_estimate=pl.CostEstimate(flops=10**8, bytes_accessed=10**8, transcendentals=0),
    )(in_weight, out_weight, fields, cotangent)


def joint_call(scalars, packed, prob, dctx, w_full, og, give):
    dma = pltpu.SemaphoreType.DMA
    area = WIN * WIN
    return pl.pallas_call(
        joint_kernel,
        out_shape=(
            shape(give.shape, BF16),
            shape(give.shape, BF16),
            shape(give.shape, BF16),
            shape(og.shape[1:], F32),
            shape((2, MINE, area, area), F32),
        ),
        in_specs=[pl.BlockSpec(memory_space=pltpu.SMEM)] + whole(6),
        out_specs=tuple(whole(5)),
        scratch_shapes=[
            pltpu.VMEM((BAND, 3 * HALF), BF16),
            pltpu.VMEM((MINE, PAIR, PAIR), F32),
            pltpu.VMEM((SIDE, SIDE, give.shape[2]), BF16),
            pltpu.VMEM((SIDE, SIDE, give.shape[2]), BF16),
            pltpu.VMEM((8,) + og.shape[1:], BF16),
            pltpu.VMEM((2, 4) + og.shape[1:], BF16),
            pltpu.VMEM((2, 4) + og.shape[1:], BF16),
            pltpu.VMEM((4, MINE, area, area), F32),
            pltpu.VMEM((4, MINE, area, area), F32),
            dma, dma, dma, dma((2, 4)), dma((2, 4)), dma((2,)), dma((2,)), dma((4,)), dma((4,)),
        ],
        compiler_params=pltpu.CompilerParams(
            collective_id=1, has_side_effects=True, vmem_limit_bytes=VMEM_LIMIT
        ),
        cost_estimate=pl.CostEstimate(flops=10**10, bytes_accessed=2 * 10**7, transcendentals=0),
    )(scalars, packed, prob, dctx, w_full, og.reshape((4, 2) + og.shape[1:]), give)


def gathered_plain(fields, in_weight, out_weight, cotangent):
    core = lax.axis_index("fsdp") % 2
    groups = same_core_groups()
    split = in_weight.reshape(in_weight.shape[0], 3, 2, HALF)
    keep = lax.dynamic_index_in_dim(split, core, 2, False).reshape(-1, 3 * HALF)
    give = lax.dynamic_index_in_dim(split, 1 - core, 2, False).reshape(-1, 3 * HALF)
    w_chip = both_halves(keep, partner(give), core)
    w_full = lax.all_gather(w_chip, "fsdp", axis=0, tiled=True, axis_index_groups=groups)
    ow_all = lax.all_gather(out_weight, "fsdp", axis=0, tiled=True)
    normed = rowwise(norm_kernel, fields)
    x_all = both_halves(normed, partner(normed), core)
    cot_all = both_halves(cotangent, partner(cotangent), core)
    return w_full, ow_all, x_all, cot_all


def shards(fields, shifts, in_weight, out_weight, bias_table, cotangent):
    row_count, col_count, width = fields.shape
    core = lax.axis_index("fsdp") % 2
    chips = lax.axis_size("fsdp") // 2
    span = 2 * WIN - 1
    area = WIN * WIN

    gather = gathered if 2 * chips == 16 else gathered_plain
    w_full, ow_all, x_all, cot_all = gather(fields, in_weight, out_weight, cotangent)
    ow_full = ow_all.reshape(2 * HALF, width)
    x_all = x_all.reshape(SIDE, col_count, width)
    cot_all = cot_all.reshape(SIDE, col_count, width)
    joint = 2 * chips == 16
    turn = 0 * core if joint else lax.axis_index("fsdp") // 2
    scalars = jnp.concatenate([shifts, jnp.stack([core, turn])]).astype(jnp.int32)

    table = offset_table(WIN)
    own_table = lax.dynamic_slice_in_dim(bias_table, core * MINE, MINE, 0)
    bias = jnp.einsum(
        "huv,pqu,rsv->hprqs",
        own_table.reshape(MINE, span, span),
        table,
        table,
        precision=lax.Precision.HIGHEST,
    ).reshape(MINE, area, area)
    bias = jnp.tile(bias, (1, 2, 2))

    tokens = SIDE * SIDE
    blocks = BANDS * 2 * MINE
    params = pltpu.CompilerParams(vmem_limit_bytes=VMEM_LIMIT)
    smem = pl.BlockSpec(memory_space=pltpu.SMEM)
    packed, prob, dctx, a_own, a_give, og = pl.pallas_call(
        forward_kernel,
        out_shape=(
            shape((tokens, 3 * HALF), BF16),
            shape((blocks, PAIR, PAIR), F32),
            shape((tokens, HALF), BF16),
            shape(fields.shape, BF16),
            shape(fields.shape, BF16),
            shape((chips, HALF // chips, width), BF16),
        ),
        in_specs=[smem] + whole(5),
        out_specs=tuple(whole(6)),
        scratch_shapes=[pltpu.VMEM((chips, HALF // chips, width), F32)],
        compiler_params=params,
        cost_estimate=pl.CostEstimate(flops=10**10, bytes_accessed=2 * 10**7, transcendentals=10**6),
    )(scalars, x_all, cot_all, w_full, ow_full, bias)

    terms = []
    for far in range(0 if joint else chips):
        route = [
            (2 * c + k, k * chips + (c + far) % chips) for c in range(chips) for k in range(2)
        ]
        terms.append(lax.ppermute(og[far], "fsdp", route))
    if joint:
        d_own, d_got, a_got, out_grad, score = joint_call(
            scalars, packed, prob, dctx, w_full, og, a_give
        )
        attended = (a_own.astype(F32) + a_got.astype(F32)).astype(BF16)
        fields_gradient = rowwise(norm_back_kernel, fields, d_own, d_got)
        local = score.reshape(HEADS, WIN, WIN, WIN, WIN)
        table_grad = jnp.einsum(
            "hprqs,pqu,rsv->huv", local, table, table, precision=lax.Precision.HIGHEST
        ).reshape(HEADS, span * span)
        return (attended, fields_gradient, out_grad, table_grad)
    a_got = partner(a_give)

    d_own, d_give, score = pl.pallas_call(
        backward_kernel,
        out_shape=(
            shape(fields.shape, BF16),
            shape(fields.shape, BF16),
            shape((MINE, PAIR, PAIR), F32),
        ),
        in_specs=[smem] + whole(4),
        out_specs=tuple(whole(3)),
        scratch_shapes=[pltpu.VMEM((BAND, 3 * HALF), BF16)],
        compiler_params=params,
        cost_estimate=pl.CostEstimate(flops=10**10, bytes_accessed=2 * 10**7, transcendentals=10**6),
    )(scalars, packed, prob, dctx, w_full)

    d_got = partner(d_give)
    attended = (a_own.astype(F32) + a_got.astype(F32)).astype(BF16)
    fields_gradient = rowwise(norm_back_kernel, fields, d_own, d_got)
    out_grad = functools.reduce(jnp.add, [term.astype(F32) for term in terms])

    local = (score[:, :area, :area] + score[:, area:, area:]).reshape(MINE, WIN, WIN, WIN, WIN)
    own_grad = jnp.einsum(
        "hprqs,pqu,rsv->huv", local, table, table, precision=lax.Precision.HIGHEST
    ).reshape(MINE, span * span)
    padded = lax.dynamic_update_slice_in_dim(
        jnp.zeros((HEADS, span * span), F32), own_grad, core * MINE, 0
    )
    table_grad = padded
    count, stride = 2 * chips, 1
    while stride < count:
        route = [(d, d ^ stride) for d in range(count)]
        table_grad = table_grad + lax.ppermute(table_grad, "fsdp", route)
        stride *= 2
    return (attended, fields_gradient, out_grad, table_grad)


def solution(mesh):
    in_specs = (
        P(("groups", "fsdp"), None, None),
        P(),
        P("fsdp", None),
        P("fsdp", None),
        P(),
        P(("groups", "fsdp"), None, None),
    )
    out_specs = (
        P(("groups", "fsdp"), None, None),
        P(("groups", "fsdp"), None, None),
        P(("groups", "fsdp"), None),
        P("groups", None),
    )
    return jax.shard_map(shards, mesh=mesh, in_specs=in_specs, out_specs=out_specs, check_vma=False)
```
